512 devices in a mesh: rows: 128 (over x, z, core), comp: 4 (over y).
Axes of the slice: x: 4, y: 4, z: 16, core: 2. Of those that a mesh axis runs over, the one named last changes fastest.
Arguments:
- frechet: float32 [4, 512, 8, 128, 128], P('comp', 'rows'), may hold values from -0.09375 to 0.09375
- pattern: int32 [512, 8], P('rows'), may hold values from 0 to 2047, as said below
- ownership: int32 [2048], replicated, may hold values from 0 to 2047, as said below
- seismograms: float32 [4, 65536], P(None, 'rows'), may hold values from -6 to 6
- signs: int32 [4, 65536], P(None, 'rows'), may hold values from 0 to 1
Outputs:
- model: float32 [4, 262144], P('comp', 'rows')
- data_dir: float32 [65536], P('rows')
The draws below stay inside these ranges and needn't reach their ends.
Inputs may be any that keep to these rules, and one draw needn't show every extreme that they name: `pattern`: each row block names 8 different column blocks, and every column block is named by some row block. Slot s belongs to index s // 16 of rows. The stored blocks of the row blocks of one index of rows fall in groups of 4 consecutive ones (within a row block) whose slots belong to one index of rows; the groups of one index of rows go to different indices, so each index sends exactly 4 stored blocks to each of 8 indices and none to the others, and each index of rows receives from exactly 8 indices. `ownership`: each slot appears once.
All inputs are finite; a program needn't handle non-finite values.
Results may differ from the reference program's by a relative error of at most 0.0003.
Values sent between devices are 32-bit elements; how exact they have to be, the bound alone decides.
No kernel may reach another device: no remote copies, remote signals or barrier semaphores. Data moves between devices by JAX's collectives and lax.ppermute only.
A program may use at most 64 MiB of HBM per device.

```python
import jax
import jax.numpy as jnp
from jax import lax

BS = 128
NNZ = 8
RB_DEV = 4
CB_DEV = 16
CAP = 4
NCOMP = 4
NENC = 4
ITERS = 2
RBLK = 512
NCB = 2048
ROWS = 65536
N_ROWS = 128


def zone_tables(key):
    key_sigma, key_tau, key_block, key_owner = jax.random.split(key, 4)
    sigma = jax.random.permutation(key_sigma, N_ROWS).astype(jnp.int32)
    tau = jax.random.permutation(key_tau, N_ROWS).astype(jnp.int32)
    base = jnp.broadcast_to(jnp.arange(CB_DEV, dtype=jnp.int32)[None, :], (N_ROWS, CB_DEV))
    block_order = jax.random.permutation(key_block, base, axis=1, independent=True).astype(jnp.int32)
    ownership = jax.random.permutation(key_owner, NCB).astype(jnp.int32)
    inverse = jnp.argsort(ownership).astype(jnp.int32)
    row_ids = jnp.arange(RBLK, dtype=jnp.int32)[:, None]
    stored_ids = jnp.arange(NNZ, dtype=jnp.int32)[None, :]
    device = row_ids // RB_DEV
    entry = row_ids % RB_DEV * NNZ + stored_ids
    group = entry // CAP
    within = entry % CAP
    owner = sigma[(tau[device] + group) % N_ROWS]
    block = block_order[owner, (CAP * group + within) % CB_DEV]
    slot = owner * CB_DEV + block
    pattern = inverse[slot]
    return (pattern.astype(jnp.int32), ownership)


def draw_pattern(key, part):
    pattern, ownership = zone_tables(key)
    return pattern


def draw_ownership(key, part):
    pattern, ownership = zone_tables(key)
    return ownership


def with_ends(array, key, least, top_value):
    spot = [jax.random.randint(jax.random.fold_in(key, axis), (), 0, length) for axis, length in enumerate(array.shape)]
    longest = array.shape.index(max(array.shape))
    neighbour = spot[:longest] + [(spot[longest] + 1) % array.shape[longest]] + spot[longest + 1:]
    return array.at[tuple(spot)].set(least).at[tuple(neighbour)].set(top_value)


def shard_levels(rng, dims, cuts, smallest, top_value):
    factor_of, own = 1.0, jax.random.fold_in(rng, 6)
    for axis_at, parts in cuts:
        heights = jnp.exp(jax.random.uniform(jax.random.fold_in(own, axis_at), (parts,), jnp.float32, smallest / len(cuts), top_value / len(cuts)))
        factor_of = factor_of * jnp.repeat(heights, dims[axis_at] // parts).reshape([-1 if axis == axis_at else 1 for axis in range(len(dims))])
    return factor_of


def noise(rng, extent, scale, reach, cuts=(), kind=jnp.bfloat16):
    drawn = jax.random.normal(rng, extent, jnp.float32) * scale
    if len(cuts) > 0:
        drawn = shard_levels(rng, extent, cuts, -0.22, 0.18) * drawn
    return jnp.clip(drawn, min=-reach, max=reach).astype(kind)


def setup_inputs(seed: int = 0) -> dict:
    key_list = jax.random.split(jax.random.key(seed), 6)
    return {
        "frechet": noise(key_list[0], (NCOMP, RBLK, NNZ, BS, BS), (NCOMP * NNZ * BS) ** -0.5, 0.09375, ((0, 4), (1, 128)), jnp.float32),
        "pattern": draw_pattern(jax.random.fold_in(key_list[5], 71), 0),
        "ownership": draw_ownership(jax.random.fold_in(key_list[5], 71), 0),
        "seismograms": noise(key_list[3], (NENC, ROWS), 1.0, 6.0, ((1, 128),), jnp.float32),
        "signs": with_ends(jax.random.randint(key_list[4], (NENC, ROWS), 0, 2), jax.random.fold_in(key_list[4], 1), 0, 1).astype(jnp.int32),
    }


EPS = 1e-12

def norm_of(values):
    return jnp.sqrt(jnp.sum(values * values) + EPS)

def reference(frechet, pattern, ownership, seismograms, signs):
    signed = (2 * signs - 1).astype(jnp.float32)
    data = lax.optimization_barrier(jnp.sum(signed * seismograms, axis=0))
    slot = ownership[pattern]

    def forward(model_vec):
        blocks = model_vec.reshape(NCOMP, NCB, BS)
        chosen = blocks[:, slot]
        out = jnp.einsum('crkij,crkj->ri', frechet, chosen, precision=lax.Precision.HIGHEST)
        return out.reshape(ROWS)

    def adjoint(data_vec):
        pieces = data_vec.reshape(RBLK, BS)
        terms = jnp.einsum('crkij,ri->crkj', frechet, pieces, precision=lax.Precision.HIGHEST)
        total = jnp.zeros((NCOMP, NCB, BS), jnp.float32).at[:, slot].add(terms)
        return total.reshape(NCOMP, NCB * BS)
    beta = norm_of(data)
    u_vec = data / beta
    v_vec = adjoint(u_vec)
    alpha = norm_of(v_vec)
    v_vec = v_vec / alpha
    w_vec = v_vec
    model = jnp.zeros((NCOMP, NCB * BS), jnp.float32)
    phibar = beta
    rhobar = alpha
    for step in range(ITERS):
        u_vec = forward(v_vec) - alpha * u_vec
        beta = norm_of(u_vec)
        u_vec = u_vec / beta
        v_vec = adjoint(u_vec) - beta * v_vec
        alpha = norm_of(v_vec)
        v_vec = v_vec / alpha
        rho = jnp.sqrt(rhobar * rhobar + beta * beta)
        cosine = rhobar / rho
        sine = beta / rho
        theta = sine * alpha
        rhobar = -cosine * alpha
        phi = cosine * phibar
        phibar = sine * phibar
        model = model + phi / rho * w_vec
        w_vec = v_vec - theta / rho * w_vec
    return (model, u_vec)
```

```python
import jax
import jax.numpy as jnp
from jax import lax
from jax.experimental import pallas as pl
from jax.experimental.pallas import tpu as pltpu
from jax.sharding import Mesh
from jax.sharding import PartitionSpec as P

EPS = 1e-12
F32 = jnp.float32
BF16 = jnp.bfloat16

X, Z, CORE, Y = 4, 16, 2, 4
ROWS = ("x", "z", "core")
PLANE = ("x", "core")
N_PLANE = X * CORE
N_ROWS = X * Z * CORE

BS = 128
RB = 4
NNZ = 8
ENTRIES = RB * NNZ
OWN = 16
WANT = ENTRIES + OWN
ZCH = ENTRIES + 1
PCH = WANT + 8
GROUPS = BS // ENTRIES
DOTS = 9

VMEM = pl.BlockSpec(memory_space=pltpu.VMEM)
SMEM = pl.BlockSpec(memory_space=pltpu.SMEM)


def call(kernel, outs, ins, scratch=(), flops=0, moved=0):
    return pl.pallas_call(
        kernel,
        out_shape=tuple(jax.ShapeDtypeStruct(s, F32) for s in outs),
        in_specs=list(ins),
        out_specs=tuple(VMEM for _ in outs),
        scratch_shapes=list(scratch),
        compiler_params=pltpu.CompilerParams(vmem_limit_bytes=32 * 1024 * 1024),
        cost_estimate=pl.CostEstimate(flops=flops, bytes_accessed=moved, transcendentals=0),
    )


def two_sum(a, b):
    s = a + b
    bb = s - a
    return s, (a - (s - bb)) + (b - bb)


def halves(a):
    c = a * 4097.0
    high = c - (c - a)
    return high, a - high


def two_prod(a, b):
    p = a * b
    ah, al = halves(a)
    bh, bl = halves(b)
    return p, ((ah * bh - p) + ah * bl + al * bh) + al * bl


def dd_add(a, b):
    s, e = two_sum(a[0], b[0])
    e = e + (a[1] + b[1])
    h = s + e
    return h, e - (h - s)


def dd_mul(a, b):
    p, e = two_prod(a[0], b[0])
    e = e + (a[0] * b[1] + a[1] * b[0])
    h = p + e
    return h, e - (h - p)


def dd_scale(a, f):
    return a[0] * f, a[1] * f


def fold_rows(pair):
    n = pair[0].shape[0]
    while n > 1:
        n //= 2
        pair = dd_add((pair[0][:n], pair[1][:n]), (pair[0][n:], pair[1][n:]))
    return pair


def dot_rows(a, b):
    return fold_rows(two_prod(a, b))


def ids_kernel(pat, own, me, bmsg, idrow):
    sub = lax.broadcasted_iota(jnp.int32, (ENTRIES, BS), 0)
    lane = lax.broadcasted_iota(jnp.int32, (8, BS), 1) - me[1] * ENTRIES
    col = jnp.zeros((ENTRIES, BS), jnp.int32)
    row = jnp.full((8, BS), -1, jnp.int32)
    for e in range(ENTRIES):
        s = own[pat[e]]
        col = jnp.where(sub == e, s, col)
        row = jnp.where(lane == e, s, row)
    mine = me[0] * OWN + lax.broadcasted_iota(jnp.int32, (OWN, BS), 0)
    col = col.astype(F32)
    mine = mine.astype(F32)
    for i in range(N_PLANE):
        bmsg[i * WANT : i * WANT + ENTRIES, :] = col
        bmsg[i * WANT + ENTRIES : (i + 1) * WANT, :] = mine
    idrow[...] = row.astype(F32)


def adjoint_terms(blocks, u_rows, msg, extra, zmsg):
    for r in range(RB):
        spread = jnp.transpose(jnp.broadcast_to(u_rows[r], (BS, BS)))
        for k in range(NNZ):
            e = r * NNZ + k
            msg[e : e + 1, :] = jnp.sum(blocks[r, k] * spread, axis=0, keepdims=True)
    msg[ENTRIES : ENTRIES + 1, :] = extra
    whole = msg[0:ZCH, :]
    for z in range(Z):
        zmsg[z * ZCH : (z + 1) * ZCH, :] = whole


def forward_rows(blocks, chosen, acc):
    for r in range(RB):
        total = blocks[r, 0] * chosen[r * NNZ : r * NNZ + 1, :]
        for k in range(1, NNZ):
            e = r * NNZ + k
            total = total + blocks[r, k] * chosen[e : e + 1, :]
        acc[r * BS : (r + 1) * BS, :] = total
    sums = lax.dot_general(
        jnp.ones((8, BS), F32),
        acc[...],
        (((1,), (1,)), ((), ())),
        precision=lax.Precision.HIGHEST,
        preferred_element_type=F32,
    )
    return [sums[0:1, r * BS : (r + 1) * BS] for r in range(RB)]


def first_kernel(blocks, seis, signs, idrow, data, zmsg, msg):
    signed = (2 * signs[...] - 1).astype(F32) * seis[...]
    whole = jnp.sum(signed, axis=0, keepdims=True)
    rows = [whole[:, r * BS : (r + 1) * BS] for r in range(RB)]
    for r in range(RB):
        data[r : r + 1, :] = rows[r]
    square = jnp.sum(whole * whole, axis=1, keepdims=True)
    ids = idrow[0:1, :]
    adjoint_terms(blocks, rows, msg, jnp.where(ids < 0.0, square, ids), zmsg)


def select_sum(arrived, ids, wanted, pmsg, extra):
    terms = jnp.concatenate([arrived[z * ZCH : z * ZCH + ENTRIES, :] for z in range(Z)], axis=0)
    high = terms.astype(BF16)
    rest = terms - high.astype(F32)
    mid = rest.astype(BF16)
    low = (rest - mid.astype(F32)).astype(BF16)
    pick = jnp.concatenate(
        [jnp.where(wanted[...] == ids[t : t + 1, :], 1.0, 0.0).astype(BF16) for t in range(Z * ENTRIES // BS)], axis=1
    )
    sums = jnp.dot(pick, low, preferred_element_type=F32)
    sums = sums + jnp.dot(pick, mid, preferred_element_type=F32)
    sums = sums + jnp.dot(pick, high, preferred_element_type=F32)
    for i in range(N_PLANE):
        pmsg[i * PCH : i * PCH + WANT, :] = sums[i * WANT : (i + 1) * WANT]
        pmsg[i * PCH + WANT : (i + 1) * PCH, :] = extra


def first_select_kernel(arrived, wanted, pmsg, ids):
    lane = lax.broadcasted_iota(jnp.int32, (1, BS), 1)
    extra = jnp.zeros((1, BS), F32)
    for t in range(Z // GROUPS):
        row = jnp.zeros((1, BS), F32)
        for j in range(GROUPS):
            at = (t * GROUPS + j) * ZCH + ENTRIES
            line = arrived[at : at + 1, :]
            row = jnp.where(lane // ENTRIES == j, line, row)
            extra = extra + jnp.where(lane == (j + 1) % GROUPS * ENTRIES, line, 0.0)
        ids[t : t + 1, :] = row
    ids[Z // GROUPS : 8, :] = jnp.zeros((8 - Z // GROUPS, BS), F32)
    select_sum(arrived, ids, wanted, pmsg, jnp.broadcast_to(extra, (8, BS)))


def select_kernel(arrived, wanted, ids, pmsg):
    extra = arrived[ENTRIES : ENTRIES + 1, :]
    for z in range(1, Z):
        extra = extra + arrived[z * ZCH + ENTRIES : z * ZCH + ZCH, :]
    select_sum(arrived, ids, wanted, pmsg, jnp.broadcast_to(extra, (8, BS)))


def plane_sum(arrived):
    total = arrived[0:WANT, :]
    for i in range(1, N_PLANE):
        total = total + arrived[i * PCH : i * PCH + WANT, :]
    return total


def plane_extra(arrived):
    total = arrived[WANT : WANT + 1, :]
    for i in range(1, N_PLANE):
        total = total + arrived[i * PCH + WANT : i * PCH + WANT + 1, :]
    return jnp.sum(total, axis=1, keepdims=True)


def first_forward_kernel(blocks, arrived, data, v_raw, u_one, beta, ymsg, acc):
    beta_one = jnp.sqrt(plane_extra(arrived) + EPS)
    v = plane_sum(arrived) / beta_one
    v_raw[...] = v
    u_one[...] = data[...] / beta_one
    beta[...] = jnp.broadcast_to(beta_one, (8, BS))
    rows = forward_rows(blocks, v, acc)
    own = v[ENTRIES:WANT]
    extra = jnp.sum(own * own, axis=0, keepdims=True)
    for y in range(Y):
        for r in range(RB):
            ymsg[y * 8 + r : y * 8 + r + 1, :] = rows[r]
        ymsg[y * 8 + RB : (y + 1) * 8, :] = jnp.broadcast_to(extra, (8 - RB, BS))


def adjoint_kernel(blocks, arrived, rows_out, zmsg, msg):
    total = arrived[0:8, :]
    for y in range(1, Y):
        total = total + arrived[y * 8 : (y + 1) * 8, :]
    rows_out[...] = total
    adjoint_terms(blocks, [total[r : r + 1, :] for r in range(RB)], msg, total[RB : RB + 1, :], zmsg)


def second_forward_kernel(
    blocks, arrived, v_raw, u_one, rows_one, model_v, model_a, data_u, data_g, alpha, ymsg, acc, msg
):
    alpha_one = jnp.sqrt(plane_extra(arrived) + EPS)
    v = v_raw[...]
    a = plane_sum(arrived) / alpha_one - alpha_one * v
    g = rows_one[0:RB, :] / alpha_one
    data_g[...] = g
    data_u[...] = g - alpha_one * u_one[...]
    alpha[...] = jnp.broadcast_to(alpha_one, (8, BS))
    rows = forward_rows(blocks, a, acc)
    a_own = a[ENTRIES:WANT]
    v_own = v[ENTRIES:WANT] / alpha_one
    model_a[...] = a_own
    model_v[...] = v_own
    for r in range(RB):
        msg[r : r + 1, :] = rows[r]
    for i, pair in enumerate((dot_rows(a_own, a_own), dot_rows(a_own, v_own), dot_rows(v_own, v_own))):
        msg[RB + i : RB + i + 1, :] = pair[0]
        msg[8 + i : 8 + i + 1, :] = pair[1]
    msg[7:8, :] = jnp.zeros((1, BS), F32)
    msg[11:16, :] = jnp.zeros((5, BS), F32)
    whole = msg[...]
    for y in range(Y):
        ymsg[y * 16 : (y + 1) * 16, :] = whole


def products_kernel(arrived, data_u, data_g, data_q, rmsg, high, low):
    q = arrived[0:RB, :]
    for y in range(1, Y):
        q = q + arrived[y * 16 : y * 16 + RB, :]
    data_q[...] = q
    u = data_u[...]
    g = data_g[...]
    pairs = [dot_rows(u, u), dot_rows(q, q), dot_rows(q, g), dot_rows(q, u), dot_rows(g, g), dot_rows(g, u)]
    high[...] = jnp.zeros((16, BS), F32)
    low[...] = jnp.zeros((16, BS), F32)
    for i, pair in enumerate(pairs):
        high[i : i + 1, :] = pair[0]
        low[i : i + 1, :] = pair[1]
    model = (arrived[RB : RB + 3, :], arrived[8:11, :])
    for y in range(1, Y):
        at = y * 16
        model = dd_add(model, (arrived[at + RB : at + RB + 3, :], arrived[at + 8 : at + 11, :]))
    high[6:9, :] = model[0]
    low[6:9, :] = model[1]
    pair = (high[...], low[...])
    step = BS // 2
    while step:
        pair = dd_add(pair, (pltpu.roll(pair[0], step, 1), pltpu.roll(pair[1], step, 1)))
        step //= 2
    lane = lax.broadcasted_iota(jnp.int32, (16, BS), 1)
    sub = lax.broadcasted_iota(jnp.int32, (16, BS), 0)
    line = jnp.where(lane == sub, pair[0], 0.0) + jnp.where(lane == sub + 64, pair[1], 0.0)
    line = jnp.sum(line, axis=0, keepdims=True)
    rmsg[...] = jnp.broadcast_to(line, (N_ROWS, BS))


def last_kernel(arrived, beta, alpha, model_v, model_a, data_u, data_g, data_q, model, data_dir):
    total = arrived[...]
    pair = fold_rows((total, jnp.zeros_like(total)))
    lane = lax.broadcasted_iota(jnp.int32, (1, BS), 1)

    def take(line, i):
        return jnp.sum(jnp.where(lane == i, line, 0.0), axis=1, keepdims=True)

    def dot(i):
        low = take(pair[1], i) + (take(pair[0], 64 + i) + take(pair[1], 64 + i))
        return dd_add((take(pair[0], i), jnp.zeros((1, 1), F32)), (low, jnp.zeros((1, 1), F32)))

    uu, qq, qg, qu, gg, gu, aa, av, vv = [dot(i) for i in range(DOTS)]
    beta_one = beta[0:1, 0:1]
    alpha_one = alpha[0:1, 0:1]
    beta_two = jnp.sqrt(uu[0] + EPS)
    b_sq = two_prod(beta_two, beta_two)
    square = dd_add(dd_mul(b_sq, dd_add(dd_mul(b_sq, vv), dd_scale(av, -2.0))), aa)
    square = jnp.maximum(square[0] / b_sq[0], 0.0)
    alpha_two = jnp.sqrt(square + EPS)
    a_sq = two_prod(alpha_two, alpha_two)
    part = dd_add(dd_mul(b_sq, dd_add(dd_mul(b_sq, gg), dd_scale(qg, -2.0))), qq)
    part = dd_add(part, dd_mul(a_sq, dd_add(dd_mul(a_sq, uu), dd_scale(qu, -2.0))))
    part = dd_add(part, dd_scale(dd_mul(dd_mul(a_sq, b_sq), gu), 2.0))
    scale = beta_two * alpha_two
    square = jnp.maximum(part[0], 0.0) / scale / scale
    beta_three = jnp.sqrt(square + EPS)

    rho = jnp.sqrt(alpha_one * alpha_one + beta_two * beta_two)
    cosine = alpha_one / rho
    sine = beta_two / rho
    theta = sine * alpha_two
    rhobar = -cosine * alpha_two
    phi = cosine * beta_one
    phibar = sine * beta_one
    v_one = model_v[...]
    v_two = (model_a[...] / beta_two - beta_two * v_one) / alpha_two
    found = phi / rho * v_one
    w = v_two - theta / rho * v_one
    rho = jnp.sqrt(rhobar * rhobar + beta_three * beta_three)
    phi = rhobar / rho * phibar
    model[...] = found + phi / rho * w
    u_three = (data_q[...] - b_sq[0] * data_g[...] - a_sq[0] * data_u[...]) / scale
    data_dir[...] = u_three / beta_three


def exchange(array, axes, peers):
    n = array.shape[0] // peers
    if n % 8 == 0:
        return lax.all_to_all(array.reshape(peers, n, BS), axes, 0, 0, tiled=True).reshape(array.shape)
    return lax.all_to_all(array.reshape(peers * n, 1, BS), axes, 0, 0, tiled=True).reshape(array.shape)


def last_adjoint(blocks, slot, u_vec, v_vec):
    terms = jnp.einsum("rkij,ri->rkj", blocks, u_vec, precision=lax.Precision.HIGHEST)
    targets = lax.broadcasted_iota(jnp.int32, (OWN * N_ROWS, 1), 0)
    pick = (targets == slot[None, :]).astype(F32)
    total = jnp.dot(pick, terms.reshape(ENTRIES, BS), precision=lax.Precision.HIGHEST)
    v_vec = lax.psum_scatter(total, ROWS, scatter_dimension=0, tiled=True) - v_vec
    return v_vec, jnp.sqrt(lax.psum(jnp.sum(v_vec * v_vec), ROWS + ("y",)) + EPS)


def on_device(frechet, pattern, ownership, seismograms, signs):
    blocks = frechet[0]
    place = lax.axis_index(ROWS).astype(jnp.int32)
    group = lax.axis_index("z").astype(jnp.int32) % GROUPS
    me = jnp.stack([place, group])
    size = blocks.size
    msg = pltpu.VMEM((ENTRIES + 8, BS), F32)
    acc = pltpu.VMEM((RB * BS, BS), F32)
    row4, row8 = (RB, BS), (8, BS)
    zshape, pshape = (Z * ZCH, BS), (N_PLANE * PCH, BS)
    heavy = dict(flops=2 * size, moved=4 * size)

    bmsg, idrow = call(ids_kernel, [(N_PLANE * WANT, BS), row8], [SMEM] * 3)(pattern.reshape(-1), ownership, me)
    wanted = exchange(bmsg, PLANE, N_PLANE)

    data, zmsg = call(first_kernel, [row4, zshape], [VMEM] * 4, [msg], **heavy)(blocks, seismograms, signs, idrow)
    pmsg, ids = call(first_select_kernel, [pshape, row8], [VMEM] * 2)(exchange(zmsg, "z", Z), wanted)
    v_raw, u_one, beta, ymsg = call(
        first_forward_kernel, [(WANT, BS), row4, row8, (Y * 8, BS)], [VMEM] * 3, [acc], **heavy
    )(blocks, exchange(pmsg, PLANE, N_PLANE), data)
    rows_one, zmsg = call(adjoint_kernel, [row8, zshape], [VMEM] * 2, [msg], **heavy)(blocks, exchange(ymsg, "y", Y))
    (pmsg,) = call(select_kernel, [pshape], [VMEM] * 3)(exchange(zmsg, "z", Z), wanted, ids)
    model_v, model_a, data_u, data_g, alpha, ymsg = call(
        second_forward_kernel,
        [(OWN, BS), (OWN, BS), row4, row4, row8, (Y * 16, BS)],
        [VMEM] * 5,
        [acc, pltpu.VMEM((16, BS), F32)],
        **heavy,
    )(blocks, exchange(pmsg, PLANE, N_PLANE), v_raw, u_one, rows_one)
    data_q, rmsg = call(
        products_kernel, [row4, (N_ROWS, BS)], [VMEM] * 3, [pltpu.VMEM((16, BS), F32)] * 2
    )(exchange(ymsg, "y", Y), data_u, data_g)
    model, data_dir = call(last_kernel, [(OWN, BS), row4], [VMEM] * 8)(
        exchange(rmsg, ROWS, N_ROWS), beta, alpha, model_v, model_a, data_u, data_g, data_q
    )
    last_adjoint(blocks, ownership[pattern.reshape(-1)], data_dir, model_v)
    return model.reshape(1, OWN * BS), data_dir.reshape(-1)


def solution(mesh):
    split = Mesh(mesh.devices.reshape(X, Z, CORE, Y), ("x", "z", "core", "y"))
    placed = (P("y", ROWS), P(ROWS), P(), P(None, ROWS), P(None, ROWS))
    return jax.shard_map(
        on_device,
        mesh=split,
        in_specs=placed,
        out_specs=(P("y", ROWS), P(ROWS)),
        check_vma=False,
    )
```

```python
import jax
import jax.numpy as jnp
from jax import lax
from jax.experimental import pallas as pl
from jax.experimental.pallas import tpu as pltpu
from jax.sharding import Mesh
from jax.sharding import PartitionSpec as P

EPS = 1e-12
F32 = jnp.float32
BF16 = jnp.bfloat16

X, Z, CORE, Y = 4, 16, 2, 4
ROWS = ("x", "z", "core")
PLANE = ("x", "core")
N_PLANE = X * CORE
N_ROWS = X * Z * CORE

BS = 128
RB = 4
NNZ = 8
ENTRIES = RB * NNZ
OWN = 16
WANT = ENTRIES + OWN
ZCH = ENTRIES + 1
PCH = WANT + 8
PRODUCTS = 12
GROUPS = BS // ENTRIES
DOTS = 9

VMEM = pl.BlockSpec(memory_space=pltpu.VMEM)
SMEM = pl.BlockSpec(memory_space=pltpu.SMEM)


def call(kernel, outs, ins, scratch=(), flops=0, moved=0):
    return pl.pallas_call(
        kernel,
        out_shape=tuple(jax.ShapeDtypeStruct(s, F32) for s in outs),
        in_specs=list(ins),
        out_specs=tuple(VMEM for _ in outs),
        scratch_shapes=list(scratch),
        compiler_params=pltpu.CompilerParams(vmem_limit_bytes=32 * 1024 * 1024),
        cost_estimate=pl.CostEstimate(flops=flops, bytes_accessed=moved, transcendentals=0),
    )


def two_sum(a, b):
    s = a + b
    bb = s - a
    return s, (a - (s - bb)) + (b - bb)


def halves(a):
    c = a * 4097.0
    high = c - (c - a)
    return high, a - high


def two_prod(a, b):
    p = a * b
    ah, al = halves(a)
    bh, bl = halves(b)
    return p, ((ah * bh - p) + ah * bl + al * bh) + al * bl


def dd_add(a, b):
    s, e = two_sum(a[0], b[0])
    e = e + (a[1] + b[1])
    h = s + e
    return h, e - (h - s)


def dd_mul(a, b):
    p, e = two_prod(a[0], b[0])
    e = e + (a[0] * b[1] + a[1] * b[0])
    h = p + e
    return h, e - (h - p)


def dd_scale(a, f):
    return a[0] * f, a[1] * f


def fold_rows(pair):
    n = pair[0].shape[0]
    while n > 1:
        n //= 2
        pair = dd_add((pair[0][:n], pair[1][:n]), (pair[0][n:], pair[1][n:]))
    return pair


def pick_row(a, i):
    row = a[0:1, :]
    for r in range(1, a.shape[0]):
        row = jnp.where(i == r, a[r : r + 1, :], row)
    return row


def dot_rows(a, b):
    return fold_rows(two_prod(a, b))


def ids_kernel(pat, own, me, bmsg, idrow):
    sub = lax.broadcasted_iota(jnp.int32, (ENTRIES, BS), 0)
    lane = lax.broadcasted_iota(jnp.int32, (8, BS), 1) - me[1] * ENTRIES
    col = jnp.zeros((ENTRIES, BS), jnp.int32)
    row = jnp.full((8, BS), -1, jnp.int32)
    for e in range(ENTRIES):
        s = own[pat[e // NNZ, e % NNZ]]
        col = jnp.where(sub == e, s, col)
        row = jnp.where(lane == e, s, row)
    mine = me[0] * OWN + lax.broadcasted_iota(jnp.int32, (OWN, BS), 0)
    col = col.astype(F32)
    mine = mine.astype(F32)
    for i in range(N_PLANE):
        bmsg[i * WANT : i * WANT + ENTRIES, :] = col
        bmsg[i * WANT + ENTRIES : (i + 1) * WANT, :] = mine
    idrow[...] = row.astype(F32)


def adjoint_terms(blocks, u_rows, msg, extra, zmsg):
    for r in range(RB):
        spread = jnp.transpose(jnp.broadcast_to(u_rows[r], (BS, BS)))
        for k in range(NNZ):
            e = r * NNZ + k
            msg[e : e + 1, :] = jnp.sum(blocks[r, k] * spread, axis=0, keepdims=True)
    msg[ENTRIES : ENTRIES + 1, :] = extra
    whole = msg[0:ZCH, :]
    for z in range(Z):
        zmsg[z * ZCH : (z + 1) * ZCH, :] = whole


def forward_rows(blocks, chosen, acc):
    for r in range(RB):
        total = blocks[r, 0] * chosen[r * NNZ : r * NNZ + 1, :]
        for k in range(1, NNZ):
            e = r * NNZ + k
            total = total + blocks[r, k] * chosen[e : e + 1, :]
        acc[r * BS : (r + 1) * BS, :] = total
    sums = lax.dot_general(
        jnp.ones((8, BS), F32),
        acc[...],
        (((1,), (1,)), ((), ())),
        precision=lax.Precision.HIGHEST,
        preferred_element_type=F32,
    )
    return [sums[0:1, r * BS : (r + 1) * BS] for r in range(RB)]


def first_kernel(blocks, seis, signs, idrow, data, zmsg, msg):
    signed = (2 * signs[...] - 1).astype(F32) * seis[...]
    whole = jnp.sum(signed, axis=0, keepdims=True)
    rows = [whole[:, r * BS : (r + 1) * BS] for r in range(RB)]
    for r in range(RB):
        data[r : r + 1, :] = rows[r]
    square = jnp.sum(whole * whole, axis=1, keepdims=True)
    ids = idrow[0:1, :]
    adjoint_terms(blocks, rows, msg, jnp.where(ids < 0.0, square, ids), zmsg)


def select_sum(arrived, ids, wanted, pmsg, extra):
    terms = jnp.concatenate([arrived[z * ZCH : z * ZCH + ENTRIES, :] for z in range(Z)], axis=0)
    high = terms.astype(BF16)
    rest = terms - high.astype(F32)
    mid = rest.astype(BF16)
    low = (rest - mid.astype(F32)).astype(BF16)
    names = wanted[...]
    pick = jnp.concatenate(
        [jnp.where(names == ids[t : t + 1, :], 1.0, 0.0).astype(BF16) for t in range(Z * ENTRIES // BS)], axis=1
    )
    sums = jnp.dot(pick, low, preferred_element_type=F32)
    sums = sums + jnp.dot(pick, mid, preferred_element_type=F32)
    sums = sums + jnp.dot(pick, high, preferred_element_type=F32)
    for i in range(N_PLANE):
        pmsg[i * PCH : i * PCH + WANT, :] = sums[i * WANT : (i + 1) * WANT]
        pmsg[i * PCH + WANT : (i + 1) * PCH, :] = extra


def first_select_kernel(arrived, wanted, pmsg, ids):
    lane = lax.broadcasted_iota(jnp.int32, (1, BS), 1)
    extra = jnp.zeros((1, BS), F32)
    for t in range(Z // GROUPS):
        row = jnp.zeros((1, BS), F32)
        for j in range(GROUPS):
            at = (t * GROUPS + j) * ZCH + ENTRIES
            line = arrived[at : at + 1, :]
            row = jnp.where(lane // ENTRIES == j, line, row)
            extra = extra + jnp.where(lane == (j + 1) % GROUPS * ENTRIES, line, 0.0)
        ids[t : t + 1, :] = row
    ids[Z // GROUPS : 8, :] = jnp.zeros((8 - Z // GROUPS, BS), F32)
    select_sum(arrived, ids, wanted, pmsg, jnp.broadcast_to(extra, (8, BS)))


def select_kernel(arrived, wanted, ids, pmsg):
    extra = arrived[ENTRIES : ENTRIES + 1, :]
    for z in range(1, Z):
        extra = extra + arrived[z * ZCH + ENTRIES : z * ZCH + ZCH, :]
    select_sum(arrived, ids, wanted, pmsg, jnp.broadcast_to(extra, (8, BS)))


def plane_sum(arrived):
    total = arrived[0:WANT, :]
    for i in range(1, N_PLANE):
        total = total + arrived[i * PCH : i * PCH + WANT, :]
    return total


def plane_extra(arrived):
    total = arrived[WANT : WANT + 1, :]
    for i in range(1, N_PLANE):
        total = total + arrived[i * PCH + WANT : i * PCH + WANT + 1, :]
    return jnp.sum(total, axis=1, keepdims=True)


def first_forward_kernel(blocks, arrived, data, v_raw, u_one, beta, ymsg, acc):
    beta_one = jnp.sqrt(plane_extra(arrived) + EPS)
    v = plane_sum(arrived) / beta_one
    v_raw[...] = v
    u_one[...] = data[...] / beta_one
    beta[...] = jnp.broadcast_to(beta_one, (8, BS))
    rows = forward_rows(blocks, v, acc)
    own = v[ENTRIES:WANT]
    extra = jnp.sum(own * own, axis=0, keepdims=True)
    for y in range(Y):
        for r in range(RB):
            ymsg[y * 8 + r : y * 8 + r + 1, :] = rows[r]
        ymsg[y * 8 + RB : (y + 1) * 8, :] = jnp.broadcast_to(extra, (8 - RB, BS))


def adjoint_kernel(blocks, arrived, rows_out, zmsg, msg):
    total = arrived[0:8, :]
    for y in range(1, Y):
        total = total + arrived[y * 8 : (y + 1) * 8, :]
    rows_out[...] = total
    adjoint_terms(blocks, [total[r : r + 1, :] for r in range(RB)], msg, total[RB : RB + 1, :], zmsg)


def second_forward_kernel(
    blocks, arrived, v_raw, u_one, rows_one, me, model_v, model_a, data_u, data_g, alpha, ymsg, acc, msg
):
    alpha_one = jnp.sqrt(plane_extra(arrived) + EPS)
    v = v_raw[...]
    a = plane_sum(arrived) / alpha_one - alpha_one * v
    g = rows_one[0:RB, :] / alpha_one
    data_g[...] = g
    u = g - alpha_one * u_one[...]
    data_u[...] = u
    alpha[...] = jnp.broadcast_to(alpha_one, (8, BS))
    rows = forward_rows(blocks, a, acc)
    a_own = a[ENTRIES:WANT]
    v_own = v[ENTRIES:WANT] / alpha_one
    model_a[...] = a_own
    model_v[...] = v_own
    for r in range(RB):
        msg[r : r + 1, :] = rows[r]
    y = me[2]
    msg[RB : RB + 1, :] = pick_row(g, y)
    msg[RB + 1 : RB + 2, :] = pick_row(u, y)
    for i, pair in enumerate((dot_rows(a_own, a_own), dot_rows(a_own, v_own), dot_rows(v_own, v_own))):
        msg[RB + 2 + i : RB + 3 + i, :] = pair[0]
        msg[RB + 5 + i : RB + 6 + i, :] = pair[1]
    whole = msg[0:PRODUCTS, :]
    for i in range(N_PLANE * Y):
        ymsg[i * PRODUCTS : (i + 1) * PRODUCTS, :] = whole


def products_kernel(arrived, me, data_q, rmsg, q_all, g_all, u_all, high, low):
    mine = jnp.zeros((RB, BS), F32)
    model = []
    for i in range(N_PLANE):
        at = i * Y * PRODUCTS
        q = arrived[at : at + RB, :]
        for y in range(1, Y):
            q = q + arrived[at + y * PRODUCTS : at + y * PRODUCTS + RB, :]
        mine = jnp.where(me[3] == i, q, mine)
        q_all[i * RB : (i + 1) * RB, :] = q
        for y in range(Y):
            source = at + y * PRODUCTS + RB
            g_all[i * RB + y : i * RB + y + 1, :] = arrived[source : source + 1, :]
            u_all[i * RB + y : i * RB + y + 1, :] = arrived[source + 1 : source + 2, :]
            model.append((arrived[source + 2 : source + 5, :], arrived[source + 5 : source + 8, :]))
    data_q[...] = mine
    q = q_all[...]
    u = u_all[...]
    g = g_all[...]
    pairs = [dot_rows(u, u), dot_rows(q, q), dot_rows(q, g), dot_rows(q, u), dot_rows(g, g), dot_rows(g, u)]
    high[...] = jnp.zeros((16, BS), F32)
    low[...] = jnp.zeros((16, BS), F32)
    for i, pair in enumerate(pairs):
        high[i : i + 1, :] = pair[0]
        low[i : i + 1, :] = pair[1]
    while len(model) > 1:
        model = [dd_add(model[i], model[i + 1]) for i in range(0, len(model), 2)]
    high[6:9, :] = model[0][0]
    low[6:9, :] = model[0][1]
    pair = (high[...], low[...])
    step = BS // 2
    while step:
        pair = dd_add(pair, (pltpu.roll(pair[0], step, 1), pltpu.roll(pair[1], step, 1)))
        step //= 2
    lane = lax.broadcasted_iota(jnp.int32, (16, BS), 1)
    sub = lax.broadcasted_iota(jnp.int32, (16, BS), 0)
    line = jnp.where(lane == sub, pair[0], 0.0) + jnp.where(lane == sub + 64, pair[1], 0.0)
    line = jnp.sum(line, axis=0, keepdims=True)
    rmsg[...] = jnp.broadcast_to(line, (Z, BS))


def last_kernel(arrived, beta, alpha, model_v, model_a, data_u, data_g, data_q, model, data_dir):
    total = arrived[...]
    pair = fold_rows((total, jnp.zeros_like(total)))
    lane = lax.broadcasted_iota(jnp.int32, (1, BS), 1)

    def take(line, i):
        return jnp.sum(jnp.where(lane == i, line, 0.0), axis=1, keepdims=True)

    def dot(i):
        low = take(pair[1], i) + (take(pair[0], 64 + i) + take(pair[1], 64 + i))
        return dd_add((take(pair[0], i), jnp.zeros((1, 1), F32)), (low, jnp.zeros((1, 1), F32)))

    uu, qq, qg, qu, gg, gu, aa, av, vv = [dot(i) for i in range(DOTS)]
    beta_one = beta[0:1, 0:1]
    alpha_one = alpha[0:1, 0:1]
    beta_two = jnp.sqrt(uu[0] + EPS)
    b_sq = two_prod(beta_two, beta_two)
    square = dd_add(dd_mul(b_sq, dd_add(dd_mul(b_sq, vv), dd_scale(av, -2.0))), aa)
    square = jnp.maximum(square[0] / b_sq[0], 0.0)
    alpha_two = jnp.sqrt(square + EPS)
    a_sq = two_prod(alpha_two, alpha_two)
    part = dd_add(dd_mul(b_sq, dd_add(dd_mul(b_sq, gg), dd_scale(qg, -2.0))), qq)
    part = dd_add(part, dd_mul(a_sq, dd_add(dd_mul(a_sq, uu), dd_scale(qu, -2.0))))
    part = dd_add(part, dd_scale(dd_mul(dd_mul(a_sq, b_sq), gu), 2.0))
    scale = beta_two * alpha_two
    square = jnp.maximum(part[0], 0.0) / scale / scale
    beta_three = jnp.sqrt(square + EPS)

    rho = jnp.sqrt(alpha_one * alpha_one + beta_two * beta_two)
    cosine = alpha_one / rho
    sine = beta_two / rho
    theta = sine * alpha_two
    rhobar = -cosine * alpha_two
    phi = cosine * beta_one
    phibar = sine * beta_one
    v_one = model_v[...]
    v_two = (model_a[...] / beta_two - beta_two * v_one) / alpha_two
    found = phi / rho * v_one
    w = v_two - theta / rho * v_one
    rho = jnp.sqrt(rhobar * rhobar + beta_three * beta_three)
    phi = rhobar / rho * phibar
    model[...] = found + phi / rho * w
    u_three = (data_q[...] - b_sq[0] * data_g[...] - a_sq[0] * data_u[...]) / scale
    data_dir[...] = u_three / beta_three


def exchange(array, axes, peers):
    n = array.shape[0] // peers
    if n % 8 == 0:
        return lax.all_to_all(array.reshape(peers, n, BS), axes, 0, 0, tiled=True).reshape(array.shape)
    return lax.all_to_all(array.reshape(peers * n, 1, BS), axes, 0, 0, tiled=True).reshape(array.shape)


def last_adjoint(blocks, slot, u_vec, v_vec):
    terms = jnp.einsum("rkij,ri->rkj", blocks, u_vec, precision=lax.Precision.HIGHEST)
    targets = lax.broadcasted_iota(jnp.int32, (OWN * N_ROWS, 1), 0)
    pick = (targets == slot[None, :]).astype(F32)
    total = jnp.dot(pick, terms.reshape(ENTRIES, BS), precision=lax.Precision.HIGHEST)
    v_vec = lax.psum_scatter(total, ROWS, scatter_dimension=0, tiled=True) - v_vec
    return v_vec, jnp.sqrt(lax.psum(jnp.sum(v_vec * v_vec), ROWS + ("y",)) + EPS)


def on_device(frechet, pattern, ownership, seismograms, signs):
    blocks = frechet[0]
    place = lax.axis_index(ROWS).astype(jnp.int32)
    group = lax.axis_index("z").astype(jnp.int32) % GROUPS
    plane = lax.axis_index(PLANE).astype(jnp.int32)
    me = jnp.stack([place, group, lax.axis_index("y").astype(jnp.int32), plane])
    size = blocks.size
    msg = pltpu.VMEM((ENTRIES + 8, BS), F32)
    acc = pltpu.VMEM((RB * BS, BS), F32)
    row4, row8 = (RB, BS), (8, BS)
    zshape, pshape = (Z * ZCH, BS), (N_PLANE * PCH, BS)
    heavy = dict(flops=2 * size, moved=4 * size)

    bmsg, idrow = call(ids_kernel, [(N_PLANE * WANT, BS), row8], [SMEM] * 3)(pattern, ownership, me)
    wanted = exchange(bmsg, PLANE, N_PLANE)

    data, zmsg = call(first_kernel, [row4, zshape], [VMEM] * 4, [msg], **heavy)(blocks, seismograms, signs, idrow)
    pmsg, ids = call(first_select_kernel, [pshape, row8], [VMEM] * 2)(exchange(zmsg, "z", Z), wanted)
    v_raw, u_one, beta, ymsg = call(
        first_forward_kernel, [(WANT, BS), row4, row8, (Y * 8, BS)], [VMEM] * 3, [acc], **heavy
    )(blocks, exchange(pmsg, PLANE, N_PLANE), data)
    rows_one, zmsg = call(adjoint_kernel, [row8, zshape], [VMEM] * 2, [msg], **heavy)(blocks, exchange(ymsg, "y", Y))
    (pmsg,) = call(select_kernel, [pshape], [VMEM] * 3)(exchange(zmsg, "z", Z), wanted, ids)
    model_v, model_a, data_u, data_g, alpha, ymsg = call(
        second_forward_kernel,
        [(OWN, BS), (OWN, BS), row4, row4, row8, (N_PLANE * Y * PRODUCTS, BS)],
        [VMEM] * 5 + [SMEM],
        [acc, pltpu.VMEM((16, BS), F32)],
        **heavy,
    )(blocks, exchange(pmsg, PLANE, N_PLANE), v_raw, u_one, rows_one, me)
    data_q, rmsg = call(
        products_kernel,
        [row4, (Z, BS)],
        [VMEM, SMEM],
        [pltpu.VMEM((N_PLANE * RB, BS), F32)] * 3 + [pltpu.VMEM((16, BS), F32)] * 2,
    )(exchange(ymsg, PLANE + ("y",), N_PLANE * Y), me)
    model, data_dir = call(last_kernel, [(OWN, BS), row4], [VMEM] * 8)(
        exchange(rmsg, "z", Z), beta, alpha, model_v, model_a, data_u, data_g, data_q
    )
    last_adjoint(blocks, ownership[pattern.reshape(-1)], data_dir, model_v)
    return model.reshape(1, OWN * BS), data_dir.reshape(-1)


def solution(mesh):
    split = Mesh(mesh.devices.reshape(X, Z, CORE, Y), ("x", "z", "core", "y"))
    placed = (P("y", ROWS), P(ROWS), P(), P(None, ROWS), P(None, ROWS))
    return jax.shard_map(
        on_device,
        mesh=split,
        in_specs=placed,
        out_specs=(P("y", ROWS), P(ROWS)),
        check_vma=False,
    )
```

```python
import jax
import jax.numpy as jnp
from jax import lax
from jax.experimental import pallas as pl
from jax.experimental.pallas import tpu as pltpu
from jax.sharding import Mesh
from jax.sharding import PartitionSpec as P

EPS = 1e-12
F32 = jnp.float32
BF16 = jnp.bfloat16

X, Z, CORE, Y = 4, 16, 2, 4
ROWS = ("x", "z", "core")
PLANE = ("x", "core")
N_PLANE = X * CORE
N_ROWS = X * Z * CORE

BS = 128
RB = 4
NNZ = 8
ENTRIES = RB * NNZ
OWN = 16
WANT = ENTRIES + OWN
ZCH = ENTRIES + 1
PCH = WANT + 8
PRODUCTS = 12
GROUPS = BS // ENTRIES
DOTS = 9

VMEM = pl.BlockSpec(memory_space=pltpu.VMEM)
SMEM = pl.BlockSpec(memory_space=pltpu.SMEM)
HBM = pl.BlockSpec(memory_space=pltpu.HBM)


def call(kernel, outs, ins, scratch=(), flops=0, moved=0, vmem=32 * 1024 * 1024):
    return pl.pallas_call(
        kernel,
        out_shape=tuple(jax.ShapeDtypeStruct(s, F32) for s in outs),
        in_specs=list(ins),
        out_specs=tuple(VMEM for _ in outs),
        scratch_shapes=list(scratch),
        compiler_params=pltpu.CompilerParams(vmem_limit_bytes=vmem),
        cost_estimate=pl.CostEstimate(flops=flops, bytes_accessed=moved, transcendentals=0),
    )


def two_sum(a, b):
    s = a + b
    bb = s - a
    return s, (a - (s - bb)) + (b - bb)


def halves(a):
    c = a * 4097.0
    high = c - (c - a)
    return high, a - high


def two_prod(a, b):
    p = a * b
    ah, al = halves(a)
    bh, bl = halves(b)
    return p, ((ah * bh - p) + ah * bl + al * bh) + al * bl


def dd_add(a, b):
    s, e = two_sum(a[0], b[0])
    e = e + (a[1] + b[1])
    h = s + e
    return h, e - (h - s)


def dd_mul(a, b):
    p, e = two_prod(a[0], b[0])
    e = e + (a[0] * b[1] + a[1] * b[0])
    h = p + e
    return h, e - (h - p)


def dd_scale(a, f):
    return a[0] * f, a[1] * f


def fold_rows(pair):
    n = pair[0].shape[0]
    while n > 1:
        n //= 2
        pair = dd_add((pair[0][:n], pair[1][:n]), (pair[0][n:], pair[1][n:]))
    return pair


def pick_row(a, i):
    row = a[0:1, :]
    for r in range(1, a.shape[0]):
        row = jnp.where(i == r, a[r : r + 1, :], row)
    return row


def dot_rows(a, b):
    return fold_rows(two_prod(a, b))


def adjoint_terms(block, u_rows, msg, extra, zmsg):
    for r in range(RB):
        spread = jnp.transpose(jnp.broadcast_to(u_rows[r], (BS, BS)))
        row = block(r)
        for k in range(NNZ):
            e = r * NNZ + k
            msg[e : e + 1, :] = jnp.sum(row[k] * spread, axis=0, keepdims=True)
    msg[ENTRIES : ENTRIES + 1, :] = extra
    whole = msg[0:ZCH, :]
    for z in range(Z):
        zmsg[z * ZCH : (z + 1) * ZCH, :] = whole


def forward_rows(blocks, chosen, acc):
    for r in range(RB):
        total = blocks[r, 0] * chosen[r * NNZ : r * NNZ + 1, :]
        for k in range(1, NNZ):
            e = r * NNZ + k
            total = total + blocks[r, k] * chosen[e : e + 1, :]
        acc[r * BS : (r + 1) * BS, :] = total
    sums = lax.dot_general(
        jnp.ones((8, BS), F32),
        acc[...],
        (((1,), (1,)), ((), ())),
        precision=lax.Precision.HIGHEST,
        preferred_element_type=F32,
    )
    return [sums[0:1, r * BS : (r + 1) * BS] for r in range(RB)]


def first_kernel(
    blocks, seis, signs, pat, own, data, zmsg, named, msg, held, seis_v, signs_v, pat_s, own_s, sems, block_sems
):
    small = [
        pltpu.make_async_copy(src, dst, sems.at[i])
        for i, (src, dst) in enumerate(((pat, pat_s), (own, own_s), (seis, seis_v), (signs, signs_v)))
    ]
    large = [pltpu.make_async_copy(blocks.at[r], held.at[r], block_sems.at[r]) for r in range(RB)]
    for copy in small + large:
        copy.start()
    small[2].wait()
    small[3].wait()
    signed = (2 * signs_v[...] - 1).astype(F32) * seis_v[...]
    whole = jnp.sum(signed, axis=0, keepdims=True)
    rows = [whole[:, r * BS : (r + 1) * BS] for r in range(RB)]
    for r in range(RB):
        data[r : r + 1, :] = rows[r]
    square = jnp.sum(whole * whole, axis=1, keepdims=True)

    small[0].wait()
    small[1].wait()
    sub = lax.broadcasted_iota(jnp.int32, (ENTRIES, BS), 0)
    lane = lax.broadcasted_iota(jnp.int32, (1, BS), 1) - lax.axis_index("z") % GROUPS * ENTRIES
    col = jnp.zeros((ENTRIES, BS), jnp.int32)
    row = jnp.full((1, BS), -1, jnp.int32)
    for e in range(ENTRIES):
        s = own_s[pat_s[e // NNZ, e % NNZ]]
        col = jnp.where(sub == e, s, col)
        row = jnp.where(lane == e, s, row)
    named[...] = col.astype(F32)
    ids = row.astype(F32)

    def block(r):
        large[r].wait()
        return [held[r, k] for k in range(NNZ)]

    adjoint_terms(block, rows, msg, jnp.where(ids < 0.0, square, ids), zmsg)


def select_sum(arrived, ids, named, pmsg, extra):
    terms = jnp.concatenate([arrived[z * ZCH : z * ZCH + ENTRIES, :] for z in range(Z)], axis=0)
    high = terms.astype(BF16)
    rest = terms - high.astype(F32)
    mid = rest.astype(BF16)
    low = (rest - mid.astype(F32)).astype(BF16)
    step = lax.broadcasted_iota(jnp.int32, (OWN, BS), 0)
    x_here, z_here, core_here = [lax.axis_index(axis) for axis in ROWS]
    peers, names = [], []
    for away in range(X):
        for other in range(CORE):
            x, core = (x_here + away) % X, (core_here + other) % CORE
            peers.append(x * CORE + core)
            names.append(named[away][other * ENTRIES : (other + 1) * ENTRIES, :])
            names.append((((x * Z + z_here) * CORE + core) * OWN + step).astype(F32))
    names = jnp.concatenate(names, axis=0)
    pick = jnp.concatenate(
        [jnp.where(names == ids[t : t + 1, :], 1.0, 0.0).astype(BF16) for t in range(Z * ENTRIES // BS)], axis=1
    )
    sums = jnp.dot(pick, low, preferred_element_type=F32)
    sums = sums + jnp.dot(pick, mid, preferred_element_type=F32)
    sums = sums + jnp.dot(pick, high, preferred_element_type=F32)
    for i, peer in enumerate(peers):
        at = pl.multiple_of(peer * PCH, 8)
        pmsg[pl.ds(at, WANT), :] = sums[i * WANT : (i + 1) * WANT]
        pmsg[pl.ds(at + WANT, 8), :] = extra


def first_select_kernel(arrived, n0, n1, n2, n3, pmsg, ids):
    lane = lax.broadcasted_iota(jnp.int32, (1, BS), 1)
    extra = jnp.zeros((1, BS), F32)
    for t in range(Z // GROUPS):
        row = jnp.zeros((1, BS), F32)
        for j in range(GROUPS):
            at = (t * GROUPS + j) * ZCH + ENTRIES
            line = arrived[at : at + 1, :]
            row = jnp.where(lane // ENTRIES == j, line, row)
            extra = extra + jnp.where(lane == (j + 1) % GROUPS * ENTRIES, line, 0.0)
        ids[t : t + 1, :] = row
    ids[Z // GROUPS : 8, :] = jnp.zeros((8 - Z // GROUPS, BS), F32)
    select_sum(arrived, ids, (n0, n1, n2, n3), pmsg, jnp.broadcast_to(extra, (8, BS)))


def select_kernel(arrived, n0, n1, n2, n3, ids, pmsg):
    extra = arrived[ENTRIES : ENTRIES + 1, :]
    for z in range(1, Z):
        extra = extra + arrived[z * ZCH + ENTRIES : z * ZCH + ZCH, :]
    select_sum(arrived, ids, (n0, n1, n2, n3), pmsg, jnp.broadcast_to(extra, (8, BS)))


def plane_sum(arrived):
    total = arrived[0:WANT, :]
    for i in range(1, N_PLANE):
        total = total + arrived[i * PCH : i * PCH + WANT, :]
    return total


def plane_extra(arrived):
    total = arrived[WANT : WANT + 1, :]
    for i in range(1, N_PLANE):
        total = total + arrived[i * PCH + WANT : i * PCH + WANT + 1, :]
    return jnp.sum(total, axis=1, keepdims=True)


def first_forward_kernel(blocks, arrived, v_raw, beta, ymsg, acc):
    beta_one = jnp.sqrt(plane_extra(arrived) + EPS)
    v = plane_sum(arrived) / beta_one
    v_raw[...] = v
    beta[...] = jnp.broadcast_to(beta_one, (8, BS))
    rows = forward_rows(blocks, v, acc)
    own = v[ENTRIES:WANT]
    extra = jnp.sum(own * own, axis=0, keepdims=True)
    for y in range(Y):
        for r in range(RB):
            ymsg[y * 8 + r : y * 8 + r + 1, :] = rows[r]
        ymsg[y * 8 + RB : (y + 1) * 8, :] = jnp.broadcast_to(extra, (8 - RB, BS))


def adjoint_kernel(blocks, arrived, rows_out, zmsg, msg):
    total = arrived[0:8, :]
    for y in range(1, Y):
        total = total + arrived[y * 8 : (y + 1) * 8, :]
    rows_out[...] = total
    rows = [total[r : r + 1, :] for r in range(RB)]
    adjoint_terms(lambda r: [blocks[r, k] for k in range(NNZ)], rows, msg, total[RB : RB + 1, :], zmsg)


def second_forward_kernel(
    blocks, arrived, v_raw, data, beta, rows_one, model_v, model_a, data_u, data_g, alpha, ymsg, acc, msg
):
    alpha_one = jnp.sqrt(plane_extra(arrived) + EPS)
    v = v_raw[...]
    a = plane_sum(arrived) / alpha_one - alpha_one * v
    g = rows_one[0:RB, :] / alpha_one
    data_g[...] = g
    u = g - alpha_one * (data[...] / beta[0:1, 0:1])
    data_u[...] = u
    alpha[...] = jnp.broadcast_to(alpha_one, (8, BS))
    rows = forward_rows(blocks, a, acc)
    a_own = a[ENTRIES:WANT]
    v_own = v[ENTRIES:WANT] / alpha_one
    model_a[...] = a_own
    model_v[...] = v_own
    for r in range(RB):
        msg[r : r + 1, :] = rows[r]
    y = lax.axis_index("y")
    msg[RB : RB + 1, :] = pick_row(g, y)
    msg[RB + 1 : RB + 2, :] = pick_row(u, y)
    for i, pair in enumerate((dot_rows(a_own, a_own), dot_rows(a_own, v_own), dot_rows(v_own, v_own))):
        msg[RB + 2 + i : RB + 3 + i, :] = pair[0]
        msg[RB + 5 + i : RB + 6 + i, :] = pair[1]
    msg[PRODUCTS : 2 * PRODUCTS, :] = msg[0:PRODUCTS, :]
    whole = msg[...]
    for i in range(N_PLANE * Y // 2):
        ymsg[i * 2 * PRODUCTS : (i + 1) * 2 * PRODUCTS, :] = whole


def products_kernel(arrived, data_q, rmsg, q_all, g_all, u_all, high, low):
    here = lax.axis_index("x") * CORE + lax.axis_index("core")
    mine = jnp.zeros((RB, BS), F32)
    model = []
    for i in range(N_PLANE):
        at = i * Y * PRODUCTS
        q = arrived[at : at + RB, :]
        for y in range(1, Y):
            q = q + arrived[at + y * PRODUCTS : at + y * PRODUCTS + RB, :]
        mine = jnp.where(here == i, q, mine)
        q_all[i * RB : (i + 1) * RB, :] = q
        for y in range(Y):
            source = at + y * PRODUCTS + RB
            g_all[i * RB + y : i * RB + y + 1, :] = arrived[source : source + 1, :]
            u_all[i * RB + y : i * RB + y + 1, :] = arrived[source + 1 : source + 2, :]
            model.append((arrived[source + 2 : source + 5, :], arrived[source + 5 : source + 8, :]))
    data_q[...] = mine
    q = q_all[...]
    u = u_all[...]
    g = g_all[...]
    pairs = [dot_rows(u, u), dot_rows(q, q), dot_rows(q, g), dot_rows(q, u), dot_rows(g, g), dot_rows(g, u)]
    high[...] = jnp.zeros((16, BS), F32)
    low[...] = jnp.zeros((16, BS), F32)
    for i, pair in enumerate(pairs):
        high[i : i + 1, :] = pair[0]
        low[i : i + 1, :] = pair[1]
    while len(model) > 1:
        model = [dd_add(model[i], model[i + 1]) for i in range(0, len(model), 2)]
    high[6:9, :] = model[0][0]
    low[6:9, :] = model[0][1]
    pair = (high[...], low[...])
    step = BS // 2
    while step:
        pair = dd_add(pair, (pltpu.roll(pair[0], step, 1), pltpu.roll(pair[1], step, 1)))
        step //= 2
    lane = lax.broadcasted_iota(jnp.int32, (16, BS), 1)
    sub = lax.broadcasted_iota(jnp.int32, (16, BS), 0)
    line = jnp.where(lane == sub, pair[0], 0.0) + jnp.where(lane == sub + 64, pair[1], 0.0)
    line = jnp.sum(line, axis=0, keepdims=True)
    rmsg[...] = jnp.broadcast_to(line, (Z, BS))


def last_kernel(arrived, beta, alpha, model_v, model_a, data_u, data_g, data_q, model, data_dir):
    total = arrived[...]
    pair = fold_rows((total, jnp.zeros_like(total)))
    lane = lax.broadcasted_iota(jnp.int32, (1, BS), 1)

    def take(line, i):
        return jnp.sum(jnp.where(lane == i, line, 0.0), axis=1, keepdims=True)

    def dot(i):
        low = take(pair[1], i) + (take(pair[0], 64 + i) + take(pair[1], 64 + i))
        return dd_add((take(pair[0], i), jnp.zeros((1, 1), F32)), (low, jnp.zeros((1, 1), F32)))

    uu, qq, qg, qu, gg, gu, aa, av, vv = [dot(i) for i in range(DOTS)]
    beta_one = beta[0:1, 0:1]
    alpha_one = alpha[0:1, 0:1]
    beta_two = jnp.sqrt(uu[0] + EPS)
    b_sq = two_prod(beta_two, beta_two)
    square = dd_add(dd_mul(b_sq, dd_add(dd_mul(b_sq, vv), dd_scale(av, -2.0))), aa)
    square = jnp.maximum(square[0] / b_sq[0], 0.0)
    alpha_two = jnp.sqrt(square + EPS)
    a_sq = two_prod(alpha_two, alpha_two)
    part = dd_add(dd_mul(b_sq, dd_add(dd_mul(b_sq, gg), dd_scale(qg, -2.0))), qq)
    part = dd_add(part, dd_mul(a_sq, dd_add(dd_mul(a_sq, uu), dd_scale(qu, -2.0))))
    part = dd_add(part, dd_scale(dd_mul(dd_mul(a_sq, b_sq), gu), 2.0))
    scale = beta_two * alpha_two
    square = jnp.maximum(part[0], 0.0) / scale / scale
    beta_three = jnp.sqrt(square + EPS)

    rho = jnp.sqrt(alpha_one * alpha_one + beta_two * beta_two)
    cosine = alpha_one / rho
    sine = beta_two / rho
    theta = sine * alpha_two
    rhobar = -cosine * alpha_two
    phi = cosine * beta_one
    phibar = sine * beta_one
    v_one = model_v[...]
    v_two = (model_a[...] / beta_two - beta_two * v_one) / alpha_two
    found = phi / rho * v_one
    w = v_two - theta / rho * v_one
    rho = jnp.sqrt(rhobar * rhobar + beta_three * beta_three)
    phi = rhobar / rho * phibar
    model[...] = found + phi / rho * w
    u_three = (data_q[...] - b_sq[0] * data_g[...] - a_sq[0] * data_u[...]) / scale
    data_dir[...] = u_three / beta_three


def exchange(array, axes, peers):
    n = array.shape[0] // peers
    if n % 8 == 0:
        return lax.all_to_all(array.reshape(peers, n, BS), axes, 0, 0, tiled=True).reshape(array.shape)
    return lax.all_to_all(array.reshape(peers * n, 1, BS), axes, 0, 0, tiled=True).reshape(array.shape)


def last_adjoint(blocks, slot, u_vec, v_vec):
    terms = jnp.einsum("rkij,ri->rkj", blocks, u_vec, precision=lax.Precision.HIGHEST)
    targets = lax.broadcasted_iota(jnp.int32, (OWN * N_ROWS, 1), 0)
    pick = (targets == slot[None, :]).astype(F32)
    total = jnp.dot(pick, terms.reshape(ENTRIES, BS), precision=lax.Precision.HIGHEST)
    v_vec = lax.psum_scatter(total, ROWS, scatter_dimension=0, tiled=True) - v_vec
    return v_vec, jnp.sqrt(lax.psum(jnp.sum(v_vec * v_vec), ROWS + ("y",)) + EPS)


def on_device(frechet, pattern, ownership, seismograms, signs):
    blocks = frechet[0]
    size = blocks.size
    msg = pltpu.VMEM((ENTRIES + 8, BS), F32)
    acc = pltpu.VMEM((RB * BS, BS), F32)
    row4, row8 = (RB, BS), (8, BS)
    zshape, pshape = (Z * ZCH, BS), (N_PLANE * PCH, BS)
    heavy = dict(flops=2 * size, moved=4 * size)

    data, zmsg, named = call(
        first_kernel,
        [row4, zshape, (ENTRIES, BS)],
        [HBM] * 5,
        [
            msg,
            pltpu.VMEM(blocks.shape, F32),
            pltpu.VMEM(seismograms.shape, F32),
            pltpu.VMEM(signs.shape, jnp.int32),
            pltpu.SMEM(pattern.shape, jnp.int32),
            pltpu.SMEM(ownership.shape, jnp.int32),
            pltpu.SemaphoreType.DMA((4,)),
            pltpu.SemaphoreType.DMA((RB,)),
        ],
        vmem=59 * 1024 * 1024,
        **heavy,
    )(blocks, seismograms, signs, pattern, ownership)
    arrived = exchange(zmsg, "z", Z)
    near = jnp.concatenate([named, lax.ppermute(named, "core", [(0, 1), (1, 0)])], axis=0)
    named = [near] + [lax.ppermute(near, "x", [((i + d) % X, i) for i in range(X)]) for d in range(1, X)]
    pmsg, ids = call(first_select_kernel, [pshape, row8], [VMEM] * 5)(arrived, *named)
    v_raw, beta, ymsg = call(
        first_forward_kernel, [(WANT, BS), row8, (Y * 8, BS)], [VMEM] * 2, [acc], **heavy
    )(blocks, exchange(pmsg, PLANE, N_PLANE))
    rows_one, zmsg = call(adjoint_kernel, [row8, zshape], [VMEM] * 2, [msg], **heavy)(blocks, exchange(ymsg, "y", Y))
    (pmsg,) = call(select_kernel, [pshape], [VMEM] * 6)(exchange(zmsg, "z", Z), *named, ids)
    model_v, model_a, data_u, data_g, alpha, ymsg = call(
        second_forward_kernel,
        [(OWN, BS), (OWN, BS), row4, row4, row8, (N_PLANE * Y * PRODUCTS, BS)],
        [VMEM] * 6,
        [acc, pltpu.VMEM((2 * PRODUCTS, BS), F32)],
        **heavy,
    )(blocks, exchange(pmsg, PLANE, N_PLANE), v_raw, data, beta, rows_one)
    data_q, rmsg = call(
        products_kernel,
        [row4, (Z, BS)],
        [VMEM],
        [pltpu.VMEM((N_PLANE * RB, BS), F32)] * 3 + [pltpu.VMEM((16, BS), F32)] * 2,
    )(exchange(ymsg, PLANE + ("y",), N_PLANE * Y))
    model, data_dir = call(last_kernel, [(OWN, BS), row4], [VMEM] * 8)(
        exchange(rmsg, "z", Z), beta, alpha, model_v, model_a, data_u, data_g, data_q
    )
    last_adjoint(blocks, ownership[pattern.reshape(-1)], data_dir, model_v)
    return model.reshape(1, OWN * BS), data_dir.reshape(-1)


def solution(mesh):
    split = Mesh(mesh.devices.reshape(X, Z, CORE, Y), ("x", "z", "core", "y"))
    placed = (P("y", ROWS), P(ROWS), P(), P(None, ROWS), P(None, ROWS))
    return jax.shard_map(
        on_device,
        mesh=split,
        in_specs=placed,
        out_specs=(P("y", ROWS), P(ROWS)),
        check_vma=False,
    )
```

```python
import jax
import jax.numpy as jnp
from jax import lax
from jax.experimental import pallas as pl
from jax.experimental.pallas import tpu as pltpu
from jax.sharding import Mesh
from jax.sharding import PartitionSpec as P

EPS = 1e-12
F32 = jnp.float32
BF16 = jnp.bfloat16

X, Z, CORE, Y = 4, 16, 2, 4
ROWS = ("x", "z", "core")
PLANE = ("x", "core")
N_PLANE = X * CORE
N_ROWS = X * Z * CORE

BS = 128
RB = 4
NNZ = 8
ENTRIES = RB * NNZ
OWN = 16
WANT = ENTRIES + OWN
ZCH = ENTRIES + 1
PCH = WANT + 8
PRODUCTS = 12
GROUPS = BS // ENTRIES
DOTS = 9

VMEM = pl.BlockSpec(memory_space=pltpu.VMEM)
SMEM = pl.BlockSpec(memory_space=pltpu.SMEM)
HBM = pl.BlockSpec(memory_space=pltpu.HBM)


def call(kernel, outs, ins, scratch=(), flops=0, moved=0, vmem=32 * 1024 * 1024):
    return pl.pallas_call(
        kernel,
        out_shape=tuple(jax.ShapeDtypeStruct(s, F32) for s in outs),
        in_specs=list(ins),
        out_specs=tuple(VMEM for _ in outs),
        scratch_shapes=list(scratch),
        compiler_params=pltpu.CompilerParams(vmem_limit_bytes=vmem),
        cost_estimate=pl.CostEstimate(flops=flops, bytes_accessed=moved, transcendentals=0),
    )


def two_sum(a, b):
    s = a + b
    bb = s - a
    return s, (a - (s - bb)) + (b - bb)


def halves(a):
    c = a * 4097.0
    high = c - (c - a)
    return high, a - high


def two_prod(a, b):
    p = a * b
    ah, al = halves(a)
    bh, bl = halves(b)
    return p, ((ah * bh - p) + ah * bl + al * bh) + al * bl


def dd_add(a, b):
    s, e = two_sum(a[0], b[0])
    e = e + (a[1] + b[1])
    h = s + e
    return h, e - (h - s)


def dd_mul(a, b):
    p, e = two_prod(a[0], b[0])
    e = e + (a[0] * b[1] + a[1] * b[0])
    h = p + e
    return h, e - (h - p)


def dd_scale(a, f):
    return a[0] * f, a[1] * f


def fold_rows(pair):
    n = pair[0].shape[0]
    while n > 1:
        n //= 2
        pair = dd_add((pair[0][:n], pair[1][:n]), (pair[0][n:], pair[1][n:]))
    return pair


def pick_row(a, i):
    row = a[0:1, :]
    for r in range(1, a.shape[0]):
        row = jnp.where(i == r, a[r : r + 1, :], row)
    return row


def dot_rows(a, b):
    return fold_rows(two_prod(a, b))


def adjoint_terms(block, u_rows, msg, extra, zmsg):
    for r in range(RB):
        spread = jnp.transpose(jnp.broadcast_to(u_rows[r], (BS, BS)))
        row = block(r)
        for k in range(NNZ):
            e = r * NNZ + k
            msg[e : e + 1, :] = jnp.sum(row[k] * spread, axis=0, keepdims=True)
    msg[ENTRIES : ENTRIES + 1, :] = extra
    whole = msg[0:ZCH, :]
    for z in range(Z):
        zmsg[z * ZCH : (z + 1) * ZCH, :] = whole


def forward_rows(blocks, chosen, acc):
    for r in range(RB):
        total = blocks[r, 0] * chosen[r * NNZ : r * NNZ + 1, :]
        for k in range(1, NNZ):
            e = r * NNZ + k
            total = total + blocks[r, k] * chosen[e : e + 1, :]
        acc[r * BS : (r + 1) * BS, :] = total
    sums = lax.dot_general(
        jnp.ones((8, BS), F32),
        acc[...],
        (((1,), (1,)), ((), ())),
        precision=lax.Precision.HIGHEST,
        preferred_element_type=F32,
    )
    return [sums[0:1, r * BS : (r + 1) * BS] for r in range(RB)]


def first_kernel(
    blocks, seis, signs, pat, own, data, zmsg, named, msg, held, seis_v, signs_v, pat_s, own_s, sems, block_sems
):
    small = [
        pltpu.make_async_copy(src, dst, sems.at[i])
        for i, (src, dst) in enumerate(((pat, pat_s), (own, own_s), (seis, seis_v), (signs, signs_v)))
    ]
    large = [pltpu.make_async_copy(blocks.at[r], held.at[r], block_sems.at[r]) for r in range(RB)]
    for copy in small + large:
        copy.start()
    small[2].wait()
    small[3].wait()
    signed = (2 * signs_v[...] - 1).astype(F32) * seis_v[...]
    whole = jnp.sum(signed, axis=0, keepdims=True)
    rows = [whole[:, r * BS : (r + 1) * BS] for r in range(RB)]
    for r in range(RB):
        data[r : r + 1, :] = rows[r]
    square = jnp.sum(whole * whole, axis=1, keepdims=True)

    small[0].wait()
    small[1].wait()
    sub = lax.broadcasted_iota(jnp.int32, (ENTRIES, BS), 0)
    lane = lax.broadcasted_iota(jnp.int32, (1, BS), 1) - lax.axis_index("z") % GROUPS * ENTRIES
    col = jnp.zeros((ENTRIES, BS), jnp.int32)
    row = jnp.full((1, BS), -1, jnp.int32)
    for e in range(ENTRIES):
        s = own_s[pat_s[e // NNZ, e % NNZ]]
        col = jnp.where(sub == e, s, col)
        row = jnp.where(lane == e, s, row)
    named[...] = col.astype(F32)
    ids = row.astype(F32)

    def block(r):
        large[r].wait()
        return [held[r, k] for k in range(NNZ)]

    adjoint_terms(block, rows, msg, jnp.where(ids < 0.0, square, ids), zmsg)


def select_sum(arrived, ids, wanted, pmsg, extra):
    terms = jnp.concatenate([arrived[z * ZCH : z * ZCH + ENTRIES, :] for z in range(Z)], axis=0)
    high = terms.astype(BF16)
    rest = terms - high.astype(F32)
    mid = rest.astype(BF16)
    low = (rest - mid.astype(F32)).astype(BF16)
    step = lax.broadcasted_iota(jnp.int32, (OWN, BS), 0)
    z_here = lax.axis_index("z")
    names = []
    for x in range(X):
        for core in range(CORE):
            i = x * CORE + core
            names.append(wanted[i * ENTRIES : (i + 1) * ENTRIES, :])
            names.append((((x * Z + z_here) * CORE + core) * OWN + step).astype(F32))
    names = jnp.concatenate(names, axis=0)
    pick = jnp.concatenate(
        [jnp.where(names == ids[t : t + 1, :], 1.0, 0.0).astype(BF16) for t in range(Z * ENTRIES // BS)], axis=1
    )
    sums = jnp.dot(pick, low, preferred_element_type=F32)
    sums = sums + jnp.dot(pick, mid, preferred_element_type=F32)
    sums = sums + jnp.dot(pick, high, preferred_element_type=F32)
    for i in range(N_PLANE):
        pmsg[i * PCH : i * PCH + WANT, :] = sums[i * WANT : (i + 1) * WANT]
        pmsg[i * PCH + WANT : (i + 1) * PCH, :] = extra


def first_select_kernel(arrived, wanted, pmsg, ids):
    lane = lax.broadcasted_iota(jnp.int32, (1, BS), 1)
    extra = jnp.zeros((1, BS), F32)
    for t in range(Z // GROUPS):
        row = jnp.zeros((1, BS), F32)
        for j in range(GROUPS):
            at = (t * GROUPS + j) * ZCH + ENTRIES
            line = arrived[at : at + 1, :]
            row = jnp.where(lane // ENTRIES == j, line, row)
            extra = extra + jnp.where(lane == (j + 1) % GROUPS * ENTRIES, line, 0.0)
        ids[t : t + 1, :] = row
    ids[Z // GROUPS : 8, :] = jnp.zeros((8 - Z // GROUPS, BS), F32)
    select_sum(arrived, ids, wanted, pmsg, jnp.broadcast_to(extra, (8, BS)))


def select_kernel(arrived, wanted, ids, pmsg):
    extra = arrived[ENTRIES : ENTRIES + 1, :]
    for z in range(1, Z):
        extra = extra + arrived[z * ZCH + ENTRIES : z * ZCH + ZCH, :]
    select_sum(arrived, ids, wanted, pmsg, jnp.broadcast_to(extra, (8, BS)))


def plane_sum(arrived):
    total = arrived[0:WANT, :]
    for i in range(1, N_PLANE):
        total = total + arrived[i * PCH : i * PCH + WANT, :]
    return total


def plane_extra(arrived):
    total = arrived[WANT : WANT + 1, :]
    for i in range(1, N_PLANE):
        total = total + arrived[i * PCH + WANT : i * PCH + WANT + 1, :]
    return jnp.sum(total, axis=1, keepdims=True)


def first_forward_kernel(blocks, arrived, v_raw, beta, ymsg, acc):
    beta_one = jnp.sqrt(plane_extra(arrived) + EPS)
    v = plane_sum(arrived) / beta_one
    v_raw[...] = v
    beta[...] = jnp.broadcast_to(beta_one, (8, BS))
    rows = forward_rows(blocks, v, acc)
    own = v[ENTRIES:WANT]
    extra = jnp.sum(own * own, axis=0, keepdims=True)
    for y in range(Y):
        for r in range(RB):
            ymsg[y * 8 + r : y * 8 + r + 1, :] = rows[r]
        ymsg[y * 8 + RB : (y + 1) * 8, :] = jnp.broadcast_to(extra, (8 - RB, BS))


def adjoint_kernel(blocks, arrived, rows_out, zmsg, msg):
    total = arrived[0:8, :]
    for y in range(1, Y):
        total = total + arrived[y * 8 : (y + 1) * 8, :]
    rows_out[...] = total
    rows = [total[r : r + 1, :] for r in range(RB)]
    adjoint_terms(lambda r: [blocks[r, k] for k in range(NNZ)], rows, msg, total[RB : RB + 1, :], zmsg)


def second_forward_kernel(
    blocks, arrived, v_raw, data, beta, rows_one, model_v, model_a, data_u, data_g, alpha, ymsg, acc, msg
):
    alpha_one = jnp.sqrt(plane_extra(arrived) + EPS)
    v = v_raw[...]
    a = plane_sum(arrived) / alpha_one - alpha_one * v
    g = rows_one[0:RB, :] / alpha_one
    data_g[...] = g
    u = g - alpha_one * (data[...] / beta[0:1, 0:1])
    data_u[...] = u
    alpha[...] = jnp.broadcast_to(alpha_one, (8, BS))
    rows = forward_rows(blocks, a, acc)
    a_own = a[ENTRIES:WANT]
    v_own = v[ENTRIES:WANT] / alpha_one
    model_a[...] = a_own
    model_v[...] = v_own
    for r in range(RB):
        msg[r : r + 1, :] = rows[r]
    y = lax.axis_index("y")
    msg[RB : RB + 1, :] = pick_row(g, y)
    msg[RB + 1 : RB + 2, :] = pick_row(u, y)
    for i, pair in enumerate((dot_rows(a_own, a_own), dot_rows(a_own, v_own), dot_rows(v_own, v_own))):
        msg[RB + 2 + i : RB + 3 + i, :] = pair[0]
        msg[RB + 5 + i : RB + 6 + i, :] = pair[1]
    msg[PRODUCTS : 2 * PRODUCTS, :] = msg[0:PRODUCTS, :]
    whole = msg[...]
    for i in range(N_PLANE * Y // 2):
        ymsg[i * 2 * PRODUCTS : (i + 1) * 2 * PRODUCTS, :] = whole


def products_kernel(arrived, data_q, rmsg, q_all, g_all, u_all, high, low):
    here = lax.axis_index("x") * CORE + lax.axis_index("core")
    mine = jnp.zeros((RB, BS), F32)
    model = []
    for i in range(N_PLANE):
        at = i * Y * PRODUCTS
        q = arrived[at : at + RB, :]
        for y in range(1, Y):
            q = q + arrived[at + y * PRODUCTS : at + y * PRODUCTS + RB, :]
        mine = jnp.where(here == i, q, mine)
        q_all[i * RB : (i + 1) * RB, :] = q
        for y in range(Y):
            source = at + y * PRODUCTS + RB
            g_all[i * RB + y : i * RB + y + 1, :] = arrived[source : source + 1, :]
            u_all[i * RB + y : i * RB + y + 1, :] = arrived[source + 1 : source + 2, :]
            model.append((arrived[source + 2 : source + 5, :], arrived[source + 5 : source + 8, :]))
    data_q[...] = mine
    q = q_all[...]
    u = u_all[...]
    g = g_all[...]
    pairs = [dot_rows(u, u), dot_rows(q, q), dot_rows(q, g), dot_rows(q, u), dot_rows(g, g), dot_rows(g, u)]
    high[...] = jnp.zeros((16, BS), F32)
    low[...] = jnp.zeros((16, BS), F32)
    for i, pair in enumerate(pairs):
        high[i : i + 1, :] = pair[0]
        low[i : i + 1, :] = pair[1]
    while len(model) > 1:
        model = [dd_add(model[i], model[i + 1]) for i in range(0, len(model), 2)]
    high[6:9, :] = model[0][0]
    low[6:9, :] = model[0][1]
    pair = (high[...], low[...])
    step = BS // 2
    while step:
        pair = dd_add(pair, (pltpu.roll(pair[0], step, 1), pltpu.roll(pair[1], step, 1)))
        step //= 2
    lane = lax.broadcasted_iota(jnp.int32, (16, BS), 1)
    sub = lax.broadcasted_iota(jnp.int32, (16, BS), 0)
    line = jnp.where(lane == sub, pair[0], 0.0) + jnp.where(lane == sub + 64, pair[1], 0.0)
    line = jnp.sum(line, axis=0, keepdims=True)
    rmsg[...] = jnp.broadcast_to(line, (Z, BS))


def last_kernel(arrived, beta, alpha, model_v, model_a, data_u, data_g, data_q, model, data_dir):
    total = arrived[...]
    pair = fold_rows((total, jnp.zeros_like(total)))
    lane = lax.broadcasted_iota(jnp.int32, (1, BS), 1)

    def take(line, i):
        return jnp.sum(jnp.where(lane == i, line, 0.0), axis=1, keepdims=True)

    def dot(i):
        low = take(pair[1], i) + (take(pair[0], 64 + i) + take(pair[1], 64 + i))
        return dd_add((take(pair[0], i), jnp.zeros((1, 1), F32)), (low, jnp.zeros((1, 1), F32)))

    uu, qq, qg, qu, gg, gu, aa, av, vv = [dot(i) for i in range(DOTS)]
    beta_one = beta[0:1, 0:1]
    alpha_one = alpha[0:1, 0:1]
    beta_two = jnp.sqrt(uu[0] + EPS)
    b_sq = two_prod(beta_two, beta_two)
    square = dd_add(dd_mul(b_sq, dd_add(dd_mul(b_sq, vv), dd_scale(av, -2.0))), aa)
    square = jnp.maximum(square[0] / b_sq[0], 0.0)
    alpha_two = jnp.sqrt(square + EPS)
    a_sq = two_prod(alpha_two, alpha_two)
    part = dd_add(dd_mul(b_sq, dd_add(dd_mul(b_sq, gg), dd_scale(qg, -2.0))), qq)
    part = dd_add(part, dd_mul(a_sq, dd_add(dd_mul(a_sq, uu), dd_scale(qu, -2.0))))
    part = dd_add(part, dd_scale(dd_mul(dd_mul(a_sq, b_sq), gu), 2.0))
    scale = beta_two * alpha_two
    square = jnp.maximum(part[0], 0.0) / scale / scale
    beta_three = jnp.sqrt(square + EPS)

    rho = jnp.sqrt(alpha_one * alpha_one + beta_two * beta_two)
    cosine = alpha_one / rho
    sine = beta_two / rho
    theta = sine * alpha_two
    rhobar = -cosine * alpha_two
    phi = cosine * beta_one
    phibar = sine * beta_one
    v_one = model_v[...]
    v_two = (model_a[...] / beta_two - beta_two * v_one) / alpha_two
    found = phi / rho * v_one
    w = v_two - theta / rho * v_one
    rho = jnp.sqrt(rhobar * rhobar + beta_three * beta_three)
    phi = rhobar / rho * phibar
    model[...] = found + phi / rho * w
    u_three = (data_q[...] - b_sq[0] * data_g[...] - a_sq[0] * data_u[...]) / scale
    data_dir[...] = u_three / beta_three


def exchange(array, axes, peers):
    n = array.shape[0] // peers
    if n % 8 == 0:
        return lax.all_to_all(array.reshape(peers, n, BS), axes, 0, 0, tiled=True).reshape(array.shape)
    return lax.all_to_all(array.reshape(peers * n, 1, BS), axes, 0, 0, tiled=True).reshape(array.shape)


def last_adjoint(blocks, slot, u_vec, v_vec):
    terms = jnp.einsum("rkij,ri->rkj", blocks, u_vec, precision=lax.Precision.HIGHEST)
    targets = lax.broadcasted_iota(jnp.int32, (OWN * N_ROWS, 1), 0)
    pick = (targets == slot[None, :]).astype(F32)
    total = jnp.dot(pick, terms.reshape(ENTRIES, BS), precision=lax.Precision.HIGHEST)
    v_vec = lax.psum_scatter(total, ROWS, scatter_dimension=0, tiled=True) - v_vec
    return v_vec, jnp.sqrt(lax.psum(jnp.sum(v_vec * v_vec), ROWS + ("y",)) + EPS)


def on_device(frechet, pattern, ownership, seismograms, signs):
    blocks = frechet[0]
    size = blocks.size
    msg = pltpu.VMEM((ENTRIES + 8, BS), F32)
    acc = pltpu.VMEM((RB * BS, BS), F32)
    row4, row8 = (RB, BS), (8, BS)
    zshape, pshape = (Z * ZCH, BS), (N_PLANE * PCH, BS)
    heavy = dict(flops=2 * size, moved=4 * size)

    data, zmsg, named = call(
        first_kernel,
        [row4, zshape, (ENTRIES, BS)],
        [HBM] * 5,
        [
            msg,
            pltpu.VMEM(blocks.shape, F32),
            pltpu.VMEM(seismograms.shape, F32),
            pltpu.VMEM(signs.shape, jnp.int32),
            pltpu.SMEM(pattern.shape, jnp.int32),
            pltpu.SMEM(ownership.shape, jnp.int32),
            pltpu.SemaphoreType.DMA((4,)),
            pltpu.SemaphoreType.DMA((RB,)),
        ],
        vmem=59 * 1024 * 1024,
        **heavy,
    )(blocks, seismograms, signs, pattern, ownership)
    arrived = exchange(zmsg, "z", Z)
    wanted = lax.all_gather(named, PLANE, axis=0, tiled=True)
    pmsg, ids = call(first_select_kernel, [pshape, row8], [VMEM] * 2)(arrived, wanted)
    v_raw, beta, ymsg = call(
        first_forward_kernel, [(WANT, BS), row8, (Y * 8, BS)], [VMEM] * 2, [acc], **heavy
    )(blocks, exchange(pmsg, PLANE, N_PLANE))
    rows_one, zmsg = call(adjoint_kernel, [row8, zshape], [VMEM] * 2, [msg], **heavy)(blocks, exchange(ymsg, "y", Y))
    (pmsg,) = call(select_kernel, [pshape], [VMEM] * 3)(exchange(zmsg, "z", Z), wanted, ids)
    model_v, model_a, data_u, data_g, alpha, ymsg = call(
        second_forward_kernel,
        [(OWN, BS), (OWN, BS), row4, row4, row8, (N_PLANE * Y * PRODUCTS, BS)],
        [VMEM] * 6,
        [acc, pltpu.VMEM((2 * PRODUCTS, BS), F32)],
        **heavy,
    )(blocks, exchange(pmsg, PLANE, N_PLANE), v_raw, data, beta, rows_one)
    data_q, rmsg = call(
        products_kernel,
        [row4, (Z, BS)],
        [VMEM],
        [pltpu.VMEM((N_PLANE * RB, BS), F32)] * 3 + [pltpu.VMEM((16, BS), F32)] * 2,
    )(exchange(ymsg, PLANE + ("y",), N_PLANE * Y))
    model, data_dir = call(last_kernel, [(OWN, BS), row4], [VMEM] * 8)(
        exchange(rmsg, "z", Z), beta, alpha, model_v, model_a, data_u, data_g, data_q
    )
    last_adjoint(blocks, ownership[pattern.reshape(-1)], data_dir, model_v)
    return model.reshape(1, OWN * BS), data_dir.reshape(-1)


def solution(mesh):
    split = Mesh(mesh.devices.reshape(X, Z, CORE, Y), ("x", "z", "core", "y"))
    placed = (P("y", ROWS), P(ROWS), P(), P(None, ROWS), P(None, ROWS))
    return jax.shard_map(
        on_device,
        mesh=split,
        in_specs=placed,
        out_specs=(P("y", ROWS), P(ROWS)),
        check_vma=False,
    )
```

```python
import jax
import jax.numpy as jnp
from jax import lax
from jax.experimental import pallas as pl
from jax.experimental.pallas import tpu as pltpu
from jax.sharding import Mesh
from jax.sharding import PartitionSpec as P

EPS = 1e-12
F32 = jnp.float32
BF16 = jnp.bfloat16

X, Z, CORE, Y = 4, 16, 2, 4
ROWS = ("x", "z", "core")
PLANE = ("x", "core")
N_PLANE = X * CORE
N_ROWS = X * Z * CORE

BS = 128
RB = 4
NNZ = 8
ENTRIES = RB * NNZ
OWN = 16
WANT = ENTRIES + OWN
ZCH = ENTRIES + 1
PCH = WANT + 1
PRODUCTS = 12
PART = 2
GROUPS = BS // ENTRIES
DOTS = 9

VMEM = pl.BlockSpec(memory_space=pltpu.VMEM)
SMEM = pl.BlockSpec(memory_space=pltpu.SMEM)
HBM = pl.BlockSpec(memory_space=pltpu.HBM)


def call(kernel, outs, ins, scratch=(), flops=0, moved=0, vmem=32 * 1024 * 1024):
    return pl.pallas_call(
        kernel,
        out_shape=tuple(jax.ShapeDtypeStruct(s, F32) for s in outs),
        in_specs=list(ins),
        out_specs=tuple(VMEM for _ in outs),
        scratch_shapes=list(scratch),
        compiler_params=pltpu.CompilerParams(vmem_limit_bytes=vmem),
        cost_estimate=pl.CostEstimate(flops=flops, bytes_accessed=moved, transcendentals=0),
    )


def two_sum(a, b):
    s = a + b
    bb = s - a
    return s, (a - (s - bb)) + (b - bb)


def halves(a):
    c = a * 4097.0
    high = c - (c - a)
    return high, a - high


def two_prod(a, b):
    p = a * b
    ah, al = halves(a)
    bh, bl = halves(b)
    return p, ((ah * bh - p) + ah * bl + al * bh) + al * bl


def dd_add(a, b):
    s, e = two_sum(a[0], b[0])
    e = e + (a[1] + b[1])
    h = s + e
    return h, e - (h - s)


def dd_mul(a, b):
    p, e = two_prod(a[0], b[0])
    e = e + (a[0] * b[1] + a[1] * b[0])
    h = p + e
    return h, e - (h - p)


def dd_scale(a, f):
    return a[0] * f, a[1] * f


def fold_rows(pair):
    n = pair[0].shape[0]
    while n > 1:
        n //= 2
        pair = dd_add((pair[0][:n], pair[1][:n]), (pair[0][n:], pair[1][n:]))
    return pair


def pick_row(a, i):
    row = a[0:1, :]
    for r in range(1, a.shape[0]):
        row = jnp.where(i == r, a[r : r + 1, :], row)
    return row


def dot_rows(a, b):
    return fold_rows(two_prod(a, b))


def adjoint_terms(block, u_rows, msg, extra):
    for r in range(RB):
        spread = jnp.transpose(jnp.broadcast_to(u_rows[r], (BS, BS)))
        for k in range(NNZ):
            e = r * NNZ + k
            msg[e : e + 1, :] = jnp.sum(block(r, k) * spread, axis=0, keepdims=True)
    msg[ENTRIES : ENTRIES + 1, :] = extra


def spread_message(msg, zmsg):
    whole = msg[0:ZCH, :]
    for z in range(Z):
        zmsg[z * ZCH : (z + 1) * ZCH, :] = whole


def forward_rows(blocks, chosen, acc):
    for r in range(RB):
        total = blocks[r, 0] * chosen[r * NNZ : r * NNZ + 1, :]
        for k in range(1, NNZ):
            e = r * NNZ + k
            total = total + blocks[r, k] * chosen[e : e + 1, :]
        acc[r * BS : (r + 1) * BS, :] = total
    sums = lax.dot_general(
        jnp.ones((8, BS), F32),
        acc[...],
        (((1,), (1,)), ((), ())),
        precision=lax.Precision.HIGHEST,
        preferred_element_type=F32,
    )
    return [sums[0:1, r * BS : (r + 1) * BS] for r in range(RB)]


def first_kernel(
    blocks, seis, signs, pat, own, data, zmsg, named, msg, held, seis_v, signs_v, pat_s, own_s, sems, block_sems
):
    small = [
        pltpu.make_async_copy(src, dst, sems.at[i])
        for i, (src, dst) in enumerate(((pat, pat_s), (own, own_s), (seis, seis_v), (signs, signs_v)))
    ]
    large = [
        pltpu.make_async_copy(blocks.at[pl.ds(r, PART)], held.at[pl.ds(r, PART)], block_sems.at[r // PART])
        for r in range(0, RB, PART)
    ]
    for copy in small + large:
        copy.start()
    small[2].wait()
    small[3].wait()
    signed = (2 * signs_v[...] - 1).astype(F32) * seis_v[...]
    whole = jnp.sum(signed, axis=0, keepdims=True)
    rows = [whole[:, r * BS : (r + 1) * BS] for r in range(RB)]
    for r in range(RB):
        data[r : r + 1, :] = rows[r]
    square = jnp.sum(whole * whole, axis=1, keepdims=True)

    small[0].wait()
    small[1].wait()
    sub = lax.broadcasted_iota(jnp.int32, (ENTRIES, BS), 0)
    lane = lax.broadcasted_iota(jnp.int32, (1, BS), 1) - lax.axis_index("z") % GROUPS * ENTRIES
    col = jnp.zeros((ENTRIES, BS), jnp.int32)
    row = jnp.full((1, BS), -1, jnp.int32)
    for e in range(ENTRIES):
        s = own_s[pat_s[e // NNZ, e % NNZ]]
        col = jnp.where(sub == e, s, col)
        row = jnp.where(lane == e, s, row)
    named[...] = col.astype(F32)
    ids = row.astype(F32)

    def block(r, k):
        if k == 0 and r % PART == 0:
            large[r // PART].wait()
        return held[r, k]

    adjoint_terms(block, rows, msg, jnp.where(ids < 0.0, square, ids))
    spread_message(msg, zmsg)


def select_sum(arrived, ids, wanted, pmsg, extra):
    terms = jnp.concatenate([arrived[z * ZCH : z * ZCH + ENTRIES, :] for z in range(Z)], axis=0)
    high = terms.astype(BF16)
    rest = terms - high.astype(F32)
    mid = rest.astype(BF16)
    low = (rest - mid.astype(F32)).astype(BF16)
    step = lax.broadcasted_iota(jnp.int32, (OWN, BS), 0)
    z_here = lax.axis_index("z")
    names = []
    for x in range(X):
        for core in range(CORE):
            i = x * CORE + core
            names.append(wanted[i * ENTRIES : (i + 1) * ENTRIES, :])
            names.append((((x * Z + z_here) * CORE + core) * OWN + step).astype(F32))
    names = jnp.concatenate(names, axis=0)
    pick = jnp.concatenate(
        [jnp.where(names == ids[t : t + 1, :], 1.0, 0.0).astype(BF16) for t in range(Z * ENTRIES // BS)], axis=1
    )
    sums = jnp.dot(pick, low, preferred_element_type=F32)
    sums = sums + jnp.dot(pick, mid, preferred_element_type=F32)
    sums = sums + jnp.dot(pick, high, preferred_element_type=F32)
    for i in range(N_PLANE):
        pmsg[i * PCH : i * PCH + WANT, :] = sums[i * WANT : (i + 1) * WANT]
        pmsg[i * PCH + WANT : (i + 1) * PCH, :] = extra[0:1, :]


def first_select_kernel(arrived, wanted, pmsg, ids):
    lane = lax.broadcasted_iota(jnp.int32, (1, BS), 1)
    extra = jnp.zeros((1, BS), F32)
    for t in range(Z // GROUPS):
        row = jnp.zeros((1, BS), F32)
        for j in range(GROUPS):
            at = (t * GROUPS + j) * ZCH + ENTRIES
            line = arrived[at : at + 1, :]
            row = jnp.where(lane // ENTRIES == j, line, row)
            extra = extra + jnp.where(lane == (j + 1) % GROUPS * ENTRIES, line, 0.0)
        ids[t : t + 1, :] = row
    ids[Z // GROUPS : 8, :] = jnp.zeros((8 - Z // GROUPS, BS), F32)
    select_sum(arrived, ids, wanted, pmsg, jnp.broadcast_to(extra, (8, BS)))


def select_kernel(arrived, wanted, ids, pmsg):
    extra = arrived[ENTRIES : ENTRIES + 1, :]
    for z in range(1, Z):
        extra = extra + arrived[z * ZCH + ENTRIES : z * ZCH + ZCH, :]
    select_sum(arrived, ids, wanted, pmsg, jnp.broadcast_to(extra, (8, BS)))


def plane_sum(arrived):
    total = arrived[0:WANT, :]
    for i in range(1, N_PLANE):
        total = total + arrived[i * PCH : i * PCH + WANT, :]
    return total


def plane_extra(arrived):
    total = arrived[WANT : WANT + 1, :]
    for i in range(1, N_PLANE):
        total = total + arrived[i * PCH + WANT : i * PCH + WANT + 1, :]
    return jnp.sum(total, axis=1, keepdims=True)


def first_forward_kernel(blocks, arrived, v_raw, beta, ymsg, acc):
    beta_one = jnp.sqrt(plane_extra(arrived) + EPS)
    v = plane_sum(arrived) / beta_one
    v_raw[...] = v
    beta[...] = jnp.broadcast_to(beta_one, (8, BS))
    rows = forward_rows(blocks, v, acc)
    own = v[ENTRIES:WANT]
    extra = jnp.sum(own * own, axis=0, keepdims=True)
    for y in range(Y):
        for r in range(RB):
            ymsg[y * 8 + r : y * 8 + r + 1, :] = rows[r]
        ymsg[y * 8 + RB : (y + 1) * 8, :] = jnp.broadcast_to(extra, (8 - RB, BS))


def adjoint_kernel(blocks, arrived, rows_out, zmsg, msg):
    total = arrived[0:8, :]
    for y in range(1, Y):
        total = total + arrived[y * 8 : (y + 1) * 8, :]
    rows_out[...] = total
    rows = [total[r : r + 1, :] for r in range(RB)]
    adjoint_terms(lambda r, k: blocks[r, k], rows, msg, total[RB : RB + 1, :])
    spread_message(msg, zmsg)


def second_forward_kernel(
    blocks, arrived, v_raw, data, beta, rows_one, model_v, model_a, data_u, data_g, alpha, ymsg, acc, msg
):
    alpha_one = jnp.sqrt(plane_extra(arrived) + EPS)
    v = v_raw[...]
    a = plane_sum(arrived) / alpha_one - alpha_one * v
    g = rows_one[0:RB, :] / alpha_one
    data_g[...] = g
    u = g - alpha_one * (data[...] / beta[0:1, 0:1])
    data_u[...] = u
    alpha[...] = jnp.broadcast_to(alpha_one, (8, BS))
    rows = forward_rows(blocks, a, acc)
    a_own = a[ENTRIES:WANT]
    v_own = v[ENTRIES:WANT] / alpha_one
    model_a[...] = a_own
    model_v[...] = v_own
    for r in range(RB):
        msg[r : r + 1, :] = rows[r]
    y = lax.axis_index("y")
    msg[RB : RB + 1, :] = pick_row(g, y)
    msg[RB + 1 : RB + 2, :] = pick_row(u, y)
    for i, pair in enumerate((dot_rows(a_own, a_own), dot_rows(a_own, v_own), dot_rows(v_own, v_own))):
        msg[RB + 2 + i : RB + 3 + i, :] = pair[0]
        msg[RB + 5 + i : RB + 6 + i, :] = pair[1]
    msg[PRODUCTS : 2 * PRODUCTS, :] = msg[0:PRODUCTS, :]
    whole = msg[...]
    for i in range(N_PLANE * Y // 2):
        ymsg[i * 2 * PRODUCTS : (i + 1) * 2 * PRODUCTS, :] = whole


def products_kernel(arrived, data_q, rmsg, q_all, g_all, u_all, high, low):
    here = lax.axis_index("x") * CORE + lax.axis_index("core")
    mine = jnp.zeros((RB, BS), F32)
    model = []
    for i in range(N_PLANE):
        at = i * Y * PRODUCTS
        q = arrived[at : at + RB, :]
        for y in range(1, Y):
            q = q + arrived[at + y * PRODUCTS : at + y * PRODUCTS + RB, :]
        mine = jnp.where(here == i, q, mine)
        q_all[i * RB : (i + 1) * RB, :] = q
        for y in range(Y):
            source = at + y * PRODUCTS + RB
            g_all[i * RB + y : i * RB + y + 1, :] = arrived[source : source + 1, :]
            u_all[i * RB + y : i * RB + y + 1, :] = arrived[source + 1 : source + 2, :]
            model.append((arrived[source + 2 : source + 5, :], arrived[source + 5 : source + 8, :]))
    data_q[...] = mine
    q = q_all[...]
    u = u_all[...]
    g = g_all[...]
    pairs = [dot_rows(u, u), dot_rows(q, q), dot_rows(q, g), dot_rows(q, u), dot_rows(g, g), dot_rows(g, u)]
    high[...] = jnp.zeros((16, BS), F32)
    low[...] = jnp.zeros((16, BS), F32)
    for i, pair in enumerate(pairs):
        high[i : i + 1, :] = pair[0]
        low[i : i + 1, :] = pair[1]
    while len(model) > 1:
        model = [dd_add(model[i], model[i + 1]) for i in range(0, len(model), 2)]
    high[6:9, :] = model[0][0]
    low[6:9, :] = model[0][1]
    pair = (high[...], low[...])
    step = BS // 2
    while step:
        pair = dd_add(pair, (pltpu.roll(pair[0], step, 1), pltpu.roll(pair[1], step, 1)))
        step //= 2
    lane = lax.broadcasted_iota(jnp.int32, (16, BS), 1)
    sub = lax.broadcasted_iota(jnp.int32, (16, BS), 0)
    line = jnp.where(lane == sub, pair[0], 0.0) + jnp.where(lane == sub + 64, pair[1], 0.0)
    line = jnp.sum(line, axis=0, keepdims=True)
    rmsg[...] = jnp.broadcast_to(line, (Z, BS))


def last_kernel(arrived, beta, alpha, model_v, model_a, data_u, data_g, data_q, model, data_dir):
    total = arrived[...]
    pair = fold_rows((total, jnp.zeros_like(total)))
    lane = lax.broadcasted_iota(jnp.int32, (1, BS), 1)

    def take(line, i):
        return jnp.sum(jnp.where(lane == i, line, 0.0), axis=1, keepdims=True)

    def dot(i):
        low = take(pair[1], i) + (take(pair[0], 64 + i) + take(pair[1], 64 + i))
        return dd_add((take(pair[0], i), jnp.zeros((1, 1), F32)), (low, jnp.zeros((1, 1), F32)))

    uu, qq, qg, qu, gg, gu, aa, av, vv = [dot(i) for i in range(DOTS)]
    beta_one = beta[0:1, 0:1]
    alpha_one = alpha[0:1, 0:1]
    beta_two = jnp.sqrt(uu[0] + EPS)
    b_sq = two_prod(beta_two, beta_two)
    square = dd_add(dd_mul(b_sq, dd_add(dd_mul(b_sq, vv), dd_scale(av, -2.0))), aa)
    square = jnp.maximum(square[0] / b_sq[0], 0.0)
    alpha_two = jnp.sqrt(square + EPS)
    a_sq = two_prod(alpha_two, alpha_two)
    part = dd_add(dd_mul(b_sq, dd_add(dd_mul(b_sq, gg), dd_scale(qg, -2.0))), qq)
    part = dd_add(part, dd_mul(a_sq, dd_add(dd_mul(a_sq, uu), dd_scale(qu, -2.0))))
    part = dd_add(part, dd_scale(dd_mul(dd_mul(a_sq, b_sq), gu), 2.0))
    scale = beta_two * alpha_two
    square = jnp.maximum(part[0], 0.0) / scale / scale
    beta_three = jnp.sqrt(square + EPS)

    rho = jnp.sqrt(alpha_one * alpha_one + beta_two * beta_two)
    cosine = alpha_one / rho
    sine = beta_two / rho
    theta = sine * alpha_two
    rhobar = -cosine * alpha_two
    phi = cosine * beta_one
    phibar = sine * beta_one
    v_one = model_v[...]
    v_two = (model_a[...] / beta_two - beta_two * v_one) / alpha_two
    found = phi / rho * v_one
    w = v_two - theta / rho * v_one
    rho = jnp.sqrt(rhobar * rhobar + beta_three * beta_three)
    phi = rhobar / rho * phibar
    model[...] = found + phi / rho * w
    u_three = (data_q[...] - b_sq[0] * data_g[...] - a_sq[0] * data_u[...]) / scale
    data_dir[...] = u_three / beta_three


def exchange(array, axes, peers):
    n = array.shape[0] // peers
    if n % 8 == 0:
        return lax.all_to_all(array.reshape(peers, n, BS), axes, 0, 0, tiled=True).reshape(array.shape)
    return lax.all_to_all(array.reshape(peers * n, 1, BS), axes, 0, 0, tiled=True).reshape(array.shape)


def last_adjoint(blocks, slot, u_vec, v_vec):
    terms = jnp.einsum("rkij,ri->rkj", blocks, u_vec, precision=lax.Precision.HIGHEST)
    targets = lax.broadcasted_iota(jnp.int32, (OWN * N_ROWS, 1), 0)
    pick = (targets == slot[None, :]).astype(F32)
    total = jnp.dot(pick, terms.reshape(ENTRIES, BS), precision=lax.Precision.HIGHEST)
    v_vec = lax.psum_scatter(total, ROWS, scatter_dimension=0, tiled=True) - v_vec
    return v_vec, jnp.sqrt(lax.psum(jnp.sum(v_vec * v_vec), ROWS + ("y",)) + EPS)


def on_device(frechet, pattern, ownership, seismograms, signs):
    blocks = frechet[0]
    size = blocks.size
    msg = pltpu.VMEM((ENTRIES + 8, BS), F32)
    acc = pltpu.VMEM((RB * BS, BS), F32)
    row4, row8 = (RB, BS), (8, BS)
    zshape, pshape = (Z * ZCH, BS), (N_PLANE * PCH, BS)
    heavy = dict(flops=2 * size, moved=4 * size)

    data, zmsg, named = call(
        first_kernel,
        [row4, zshape, (ENTRIES, BS)],
        [HBM] * 5,
        [
            msg,
            pltpu.VMEM(blocks.shape, F32),
            pltpu.VMEM(seismograms.shape, F32),
            pltpu.VMEM(signs.shape, jnp.int32),
            pltpu.SMEM(pattern.shape, jnp.int32),
            pltpu.SMEM(ownership.shape, jnp.int32),
            pltpu.SemaphoreType.DMA((4,)),
            pltpu.SemaphoreType.DMA((RB // PART,)),
        ],
        vmem=59 * 1024 * 1024,
        **heavy,
    )(blocks, seismograms, signs, pattern, ownership)
    arrived = exchange(zmsg, "z", Z)
    wanted = lax.all_gather(named, PLANE, axis=0, tiled=True)
    pmsg, ids = call(first_select_kernel, [pshape, row8], [VMEM] * 2)(arrived, wanted)
    v_raw, beta, ymsg = call(
        first_forward_kernel, [(WANT, BS), row8, (Y * 8, BS)], [VMEM] * 2, [acc], **heavy
    )(blocks, exchange(pmsg, PLANE, N_PLANE))
    rows_one, zmsg = call(adjoint_kernel, [row8, zshape], [VMEM] * 2, [msg], **heavy)(blocks, exchange(ymsg, "y", Y))
    (pmsg,) = call(select_kernel, [pshape], [VMEM] * 3)(exchange(zmsg, "z", Z), wanted, ids)
    model_v, model_a, data_u, data_g, alpha, ymsg = call(
        second_forward_kernel,
        [(OWN, BS), (OWN, BS), row4, row4, row8, (N_PLANE * Y * PRODUCTS, BS)],
        [VMEM] * 6,
        [acc, pltpu.VMEM((2 * PRODUCTS, BS), F32)],
        **heavy,
    )(blocks, exchange(pmsg, PLANE, N_PLANE), v_raw, data, beta, rows_one)
    data_q, rmsg = call(
        products_kernel,
        [row4, (Z, BS)],
        [VMEM],
        [pltpu.VMEM((N_PLANE * RB, BS), F32)] * 3 + [pltpu.VMEM((16, BS), F32)] * 2,
    )(exchange(ymsg, PLANE + ("y",), N_PLANE * Y))
    model, data_dir = call(last_kernel, [(OWN, BS), row4], [VMEM] * 8)(
        exchange(rmsg, "z", Z), beta, alpha, model_v, model_a, data_u, data_g, data_q
    )
    last_adjoint(blocks, ownership[pattern.reshape(-1)], data_dir, model_v)
    return model.reshape(1, OWN * BS), data_dir.reshape(-1)


def solution(mesh):
    split = Mesh(mesh.devices.reshape(X, Z, CORE, Y), ("x", "z", "core", "y"))
    placed = (P("y", ROWS), P(ROWS), P(), P(None, ROWS), P(None, ROWS))
    return jax.shard_map(
        on_device,
        mesh=split,
        in_specs=placed,
        out_specs=(P("y", ROWS), P(ROWS)),
        check_vma=False,
    )
```

```python
import jax
import jax.numpy as jnp
from jax import lax
from jax.experimental import pallas as pl
from jax.experimental.pallas import tpu as pltpu
from jax.sharding import Mesh
from jax.sharding import PartitionSpec as P

EPS = 1e-12
F32 = jnp.float32
BF16 = jnp.bfloat16

X, Z, CORE, Y = 4, 16, 2, 4
ROWS = ("x", "z", "core")
PLANE = ("x", "core")
N_PLANE = X * CORE
N_ROWS = X * Z * CORE

BS = 128
RB = 4
NNZ = 8
ENTRIES = RB * NNZ
OWN = 16
WANT = ENTRIES + OWN
ZCH = ENTRIES + 1
PCH = WANT + 1
PRODUCTS = 12
PART = 2
GROUPS = BS // ENTRIES
DOTS = 9

VMEM = pl.BlockSpec(memory_space=pltpu.VMEM)
SMEM = pl.BlockSpec(memory_space=pltpu.SMEM)
HBM = pl.BlockSpec(memory_space=pltpu.HBM)


def call(kernel, outs, ins, scratch=(), flops=0, moved=0, vmem=32 * 1024 * 1024):
    return pl.pallas_call(
        kernel,
        out_shape=tuple(jax.ShapeDtypeStruct(s, F32) for s in outs),
        in_specs=list(ins),
        out_specs=tuple(VMEM for _ in outs),
        scratch_shapes=list(scratch),
        compiler_params=pltpu.CompilerParams(vmem_limit_bytes=vmem),
        cost_estimate=pl.CostEstimate(flops=flops, bytes_accessed=moved, transcendentals=0),
    )


def two_sum(a, b):
    s = a + b
    bb = s - a
    return s, (a - (s - bb)) + (b - bb)


def halves(a):
    c = a * 4097.0
    high = c - (c - a)
    return high, a - high


def two_prod(a, b):
    p = a * b
    ah, al = halves(a)
    bh, bl = halves(b)
    return p, ((ah * bh - p) + ah * bl + al * bh) + al * bl


def dd_add(a, b):
    s, e = two_sum(a[0], b[0])
    e = e + (a[1] + b[1])
    h = s + e
    return h, e - (h - s)


def dd_mul(a, b):
    p, e = two_prod(a[0], b[0])
    e = e + (a[0] * b[1] + a[1] * b[0])
    h = p + e
    return h, e - (h - p)


def dd_scale(a, f):
    return a[0] * f, a[1] * f


def fold_rows(pair):
    n = pair[0].shape[0]
    while n > 1:
        n //= 2
        pair = dd_add((pair[0][:n], pair[1][:n]), (pair[0][n:], pair[1][n:]))
    return pair


def pick_row(a, i):
    row = a[0:1, :]
    for r in range(1, a.shape[0]):
        row = jnp.where(i == r, a[r : r + 1, :], row)
    return row


def dot_rows(a, b):
    return fold_rows(two_prod(a, b))


def adjoint_terms(block, u_rows, msg, extra):
    for r in range(RB):
        spread = jnp.transpose(jnp.broadcast_to(u_rows[r], (BS, BS)))
        for k in range(NNZ):
            e = r * NNZ + k
            msg[e : e + 1, :] = jnp.sum(block(r, k) * spread, axis=0, keepdims=True)
    msg[ENTRIES : ENTRIES + 1, :] = extra


def spread_message(msg, zmsg):
    whole = msg[0:ZCH, :]
    for z in range(Z):
        zmsg[z * ZCH : (z + 1) * ZCH, :] = whole


def forward_rows(blocks, chosen):
    rows = []
    for r in range(RB):
        total = blocks[r, 0] * chosen[r * NNZ : r * NNZ + 1, :]
        for k in range(1, NNZ):
            e = r * NNZ + k
            total = total + blocks[r, k] * chosen[e : e + 1, :]
        rows.append(jnp.sum(jnp.transpose(total), axis=0, keepdims=True))
    return rows


def first_kernel(
    blocks, seis, signs, pat, own, data, zmsg, named, msg, held, seis_v, signs_v, pat_s, own_s, sems, block_sems
):
    small = [
        pltpu.make_async_copy(src, dst, sems.at[i])
        for i, (src, dst) in enumerate(((pat, pat_s), (own, own_s), (seis, seis_v), (signs, signs_v)))
    ]
    large = [
        pltpu.make_async_copy(blocks.at[pl.ds(r, PART)], held.at[pl.ds(r, PART)], block_sems.at[r // PART])
        for r in range(0, RB, PART)
    ]
    for copy in small + large:
        copy.start()
    small[2].wait()
    small[3].wait()
    signed = (2 * signs_v[...] - 1).astype(F32) * seis_v[...]
    whole = jnp.sum(signed, axis=0, keepdims=True)
    rows = [whole[:, r * BS : (r + 1) * BS] for r in range(RB)]
    for r in range(RB):
        data[r : r + 1, :] = rows[r]
    square = jnp.sum(whole * whole, axis=1, keepdims=True)

    small[0].wait()
    small[1].wait()
    sub = lax.broadcasted_iota(jnp.int32, (ENTRIES, BS), 0)
    lane = lax.broadcasted_iota(jnp.int32, (1, BS), 1) - lax.axis_index("z") % GROUPS * ENTRIES
    col = jnp.zeros((ENTRIES, BS), jnp.int32)
    row = jnp.full((1, BS), -1, jnp.int32)
    for e in range(ENTRIES):
        s = own_s[pat_s[e // NNZ, e % NNZ]]
        col = jnp.where(sub == e, s, col)
        row = jnp.where(lane == e, s, row)
    named[...] = col.astype(F32)
    ids = row.astype(F32)

    def block(r, k):
        if k == 0 and r % PART == 0:
            large[r // PART].wait()
        return held[r, k]

    adjoint_terms(block, rows, msg, jnp.where(ids < 0.0, square, ids))
    spread_message(msg, zmsg)


def select_sum(arrived, ids, wanted, pmsg, extra):
    terms = jnp.concatenate([arrived[z * ZCH : z * ZCH + ENTRIES, :] for z in range(Z)], axis=0)
    high = terms.astype(BF16)
    rest = terms - high.astype(F32)
    mid = rest.astype(BF16)
    low = (rest - mid.astype(F32)).astype(BF16)
    step = lax.broadcasted_iota(jnp.int32, (OWN, BS), 0)
    z_here = lax.axis_index("z")
    names = []
    for x in range(X):
        for core in range(CORE):
            i = x * CORE + core
            names.append(wanted[i * ENTRIES : (i + 1) * ENTRIES, :])
            names.append((((x * Z + z_here) * CORE + core) * OWN + step).astype(F32))
    names = jnp.concatenate(names, axis=0)
    pick = jnp.concatenate(
        [jnp.where(names == ids[t : t + 1, :], 1.0, 0.0).astype(BF16) for t in range(Z * ENTRIES // BS)], axis=1
    )
    sums = jnp.dot(pick, low, preferred_element_type=F32)
    both = jnp.dot(pick, jnp.concatenate([mid, high], axis=1), preferred_element_type=F32)
    sums = sums + both[:, :BS] + both[:, BS:]
    for i in range(N_PLANE):
        pmsg[i * PCH : i * PCH + WANT, :] = sums[i * WANT : (i + 1) * WANT]
        pmsg[i * PCH + WANT : (i + 1) * PCH, :] = extra[0:1, :]


def first_select_kernel(arrived, wanted, pmsg, ids):
    lane = lax.broadcasted_iota(jnp.int32, (1, BS), 1)
    extra = jnp.zeros((1, BS), F32)
    for t in range(Z // GROUPS):
        row = jnp.zeros((1, BS), F32)
        for j in range(GROUPS):
            at = (t * GROUPS + j) * ZCH + ENTRIES
            line = arrived[at : at + 1, :]
            row = jnp.where(lane // ENTRIES == j, line, row)
            extra = extra + jnp.where(lane == (j + 1) % GROUPS * ENTRIES, line, 0.0)
        ids[t : t + 1, :] = row
    ids[Z // GROUPS : 8, :] = jnp.zeros((8 - Z // GROUPS, BS), F32)
    select_sum(arrived, ids, wanted, pmsg, jnp.broadcast_to(extra, (8, BS)))


def select_kernel(arrived, wanted, ids, pmsg):
    extra = arrived[ENTRIES : ENTRIES + 1, :]
    for z in range(1, Z):
        extra = extra + arrived[z * ZCH + ENTRIES : z * ZCH + ZCH, :]
    select_sum(arrived, ids, wanted, pmsg, jnp.broadcast_to(extra, (8, BS)))


def plane_sum(arrived):
    total = arrived[0:WANT, :]
    for i in range(1, N_PLANE):
        total = total + arrived[i * PCH : i * PCH + WANT, :]
    return total


def plane_extra(arrived):
    total = arrived[WANT : WANT + 1, :]
    for i in range(1, N_PLANE):
        total = total + arrived[i * PCH + WANT : i * PCH + WANT + 1, :]
    return jnp.sum(total, axis=1, keepdims=True)


def first_forward_kernel(blocks, arrived, v_raw, beta, ymsg):
    beta_one = jnp.sqrt(plane_extra(arrived) + EPS)
    v = plane_sum(arrived) / beta_one
    v_raw[...] = v
    beta[...] = jnp.broadcast_to(beta_one, (8, BS))
    rows = forward_rows(blocks, v)
    own = v[ENTRIES:WANT]
    extra = jnp.sum(own * own, axis=0, keepdims=True)
    for y in range(Y):
        for r in range(RB):
            ymsg[y * 8 + r : y * 8 + r + 1, :] = rows[r]
        ymsg[y * 8 + RB : (y + 1) * 8, :] = jnp.broadcast_to(extra, (8 - RB, BS))


def adjoint_kernel(blocks, arrived, rows_out, zmsg, msg):
    total = arrived[0:8, :]
    for y in range(1, Y):
        total = total + arrived[y * 8 : (y + 1) * 8, :]
    rows_out[...] = total
    rows = [total[r : r + 1, :] for r in range(RB)]
    adjoint_terms(lambda r, k: blocks[r, k], rows, msg, total[RB : RB + 1, :])
    spread_message(msg, zmsg)


def second_forward_kernel(
    blocks, arrived, v_raw, data, beta, rows_one, model_v, model_a, data_u, data_g, alpha, ymsg, msg
):
    alpha_one = jnp.sqrt(plane_extra(arrived) + EPS)
    v = v_raw[...]
    a = plane_sum(arrived) / alpha_one - alpha_one * v
    g = rows_one[0:RB, :] / alpha_one
    data_g[...] = g
    u = g - alpha_one * (data[...] / beta[0:1, 0:1])
    data_u[...] = u
    alpha[...] = jnp.broadcast_to(alpha_one, (8, BS))
    rows = forward_rows(blocks, a)
    a_own = a[ENTRIES:WANT]
    v_own = v[ENTRIES:WANT] / alpha_one
    model_a[...] = a_own
    model_v[...] = v_own
    for r in range(RB):
        msg[r : r + 1, :] = rows[r]
    y = lax.axis_index("y")
    msg[RB : RB + 1, :] = pick_row(g, y)
    msg[RB + 1 : RB + 2, :] = pick_row(u, y)
    for i, pair in enumerate((dot_rows(a_own, a_own), dot_rows(a_own, v_own), dot_rows(v_own, v_own))):
        msg[RB + 2 + i : RB + 3 + i, :] = pair[0]
        msg[RB + 5 + i : RB + 6 + i, :] = pair[1]
    msg[PRODUCTS : 2 * PRODUCTS, :] = msg[0:PRODUCTS, :]
    whole = msg[...]
    for i in range(N_PLANE * Y // 2):
        ymsg[i * 2 * PRODUCTS : (i + 1) * 2 * PRODUCTS, :] = whole


def products_kernel(arrived, data_q, rmsg, q_all, g_all, u_all, high, low):
    here = lax.axis_index("x") * CORE + lax.axis_index("core")
    mine = jnp.zeros((RB, BS), F32)
    model = []
    for i in range(N_PLANE):
        at = i * Y * PRODUCTS
        q = arrived[at : at + RB, :]
        for y in range(1, Y):
            q = q + arrived[at + y * PRODUCTS : at + y * PRODUCTS + RB, :]
        mine = jnp.where(here == i, q, mine)
        q_all[i * RB : (i + 1) * RB, :] = q
        for y in range(Y):
            source = at + y * PRODUCTS + RB
            g_all[i * RB + y : i * RB + y + 1, :] = arrived[source : source + 1, :]
            u_all[i * RB + y : i * RB + y + 1, :] = arrived[source + 1 : source + 2, :]
            model.append((arrived[source + 2 : source + 5, :], arrived[source + 5 : source + 8, :]))
    data_q[...] = mine
    q = q_all[...]
    u = u_all[...]
    g = g_all[...]
    pairs = [dot_rows(u, u), dot_rows(q, q), dot_rows(q, g), dot_rows(q, u), dot_rows(g, g), dot_rows(g, u)]
    high[...] = jnp.zeros((BS, BS), F32)
    low[...] = jnp.zeros((BS, BS), F32)
    for i, pair in enumerate(pairs):
        high[i : i + 1, :] = pair[0]
        low[i : i + 1, :] = pair[1]
    while len(model) > 1:
        model = [dd_add(model[i], model[i + 1]) for i in range(0, len(model), 2)]
    high[6:9, :] = model[0][0]
    low[6:9, :] = model[0][1]
    pair = fold_rows((jnp.transpose(high[...]), jnp.transpose(low[...])))
    line = pair[0] + pltpu.roll(pair[1], BS // 2, 1)
    rmsg[...] = jnp.broadcast_to(line, (Z, BS))


def last_kernel(arrived, beta, alpha, model_v, model_a, data_u, data_g, data_q, model, data_dir):
    total = arrived[...]
    pair = fold_rows((total, jnp.zeros_like(total)))
    lane = lax.broadcasted_iota(jnp.int32, (1, BS), 1)

    rest = jnp.where(lane < BS // 2, pair[1], pair[0] + pair[1])

    def dot(i):
        top = jnp.sum(jnp.where(lane == i, pair[0], 0.0), axis=1, keepdims=True)
        low = jnp.sum(jnp.where(lane % (BS // 2) == i, rest, 0.0), axis=1, keepdims=True)
        return two_sum(top, low)

    uu, qq, qg, qu, gg, gu, aa, av, vv = [dot(i) for i in range(DOTS)]
    beta_one = beta[0:1, 0:1]
    alpha_one = alpha[0:1, 0:1]
    beta_two = jnp.sqrt(uu[0] + EPS)
    b_sq = two_prod(beta_two, beta_two)
    square = dd_add(dd_mul(b_sq, dd_add(dd_mul(b_sq, vv), dd_scale(av, -2.0))), aa)
    square = jnp.maximum(square[0] / b_sq[0], 0.0)
    alpha_two = jnp.sqrt(square + EPS)
    a_sq = two_prod(alpha_two, alpha_two)
    part = dd_add(dd_mul(b_sq, dd_add(dd_mul(b_sq, gg), dd_scale(qg, -2.0))), qq)
    part = dd_add(part, dd_mul(a_sq, dd_add(dd_mul(a_sq, uu), dd_scale(qu, -2.0))))
    part = dd_add(part, dd_scale(dd_mul(dd_mul(a_sq, b_sq), gu), 2.0))
    scale = beta_two * alpha_two
    square = jnp.maximum(part[0], 0.0) / scale / scale
    beta_three = jnp.sqrt(square + EPS)

    rho = jnp.sqrt(alpha_one * alpha_one + beta_two * beta_two)
    cosine = alpha_one / rho
    sine = beta_two / rho
    theta = sine * alpha_two
    rhobar = -cosine * alpha_two
    phi = cosine * beta_one
    phibar = sine * beta_one
    v_one = model_v[...]
    v_two = (model_a[...] / beta_two - beta_two * v_one) / alpha_two
    found = phi / rho * v_one
    w = v_two - theta / rho * v_one
    rho = jnp.sqrt(rhobar * rhobar + beta_three * beta_three)
    phi = rhobar / rho * phibar
    model[...] = found + phi / rho * w
    u_three = (data_q[...] - b_sq[0] * data_g[...] - a_sq[0] * data_u[...]) / scale
    data_dir[...] = u_three / beta_three


def exchange(array, axes, peers):
    n = array.shape[0] // peers
    if n % 8 == 0:
        return lax.all_to_all(array.reshape(peers, n, BS), axes, 0, 0, tiled=True).reshape(array.shape)
    return lax.all_to_all(array.reshape(peers * n, 1, BS), axes, 0, 0, tiled=True).reshape(array.shape)


def last_adjoint(blocks, slot, u_vec, v_vec):
    terms = jnp.einsum("rkij,ri->rkj", blocks, u_vec, precision=lax.Precision.HIGHEST)
    targets = lax.broadcasted_iota(jnp.int32, (OWN * N_ROWS, 1), 0)
    pick = (targets == slot[None, :]).astype(F32)
    total = jnp.dot(pick, terms.reshape(ENTRIES, BS), precision=lax.Precision.HIGHEST)
    v_vec = lax.psum_scatter(total, ROWS, scatter_dimension=0, tiled=True) - v_vec
    return v_vec, jnp.sqrt(lax.psum(jnp.sum(v_vec * v_vec), ROWS + ("y",)) + EPS)


def on_device(frechet, pattern, ownership, seismograms, signs):
    blocks = frechet[0]
    size = blocks.size
    msg = pltpu.VMEM((ENTRIES + 8, BS), F32)
    row4, row8 = (RB, BS), (8, BS)
    zshape, pshape = (Z * ZCH, BS), (N_PLANE * PCH, BS)
    heavy = dict(flops=2 * size, moved=4 * size)

    data, zmsg, named = call(
        first_kernel,
        [row4, zshape, (ENTRIES, BS)],
        [HBM] * 5,
        [
            msg,
            pltpu.VMEM(blocks.shape, F32),
            pltpu.VMEM(seismograms.shape, F32),
            pltpu.VMEM(signs.shape, jnp.int32),
            pltpu.SMEM(pattern.shape, jnp.int32),
            pltpu.SMEM(ownership.shape, jnp.int32),
            pltpu.SemaphoreType.DMA((4,)),
            pltpu.SemaphoreType.DMA((RB // PART,)),
        ],
        vmem=59 * 1024 * 1024,
        **heavy,
    )(blocks, seismograms, signs, pattern, ownership)
    arrived = exchange(zmsg, "z", Z)
    wanted = lax.all_gather(named, PLANE, axis=0, tiled=True)
    pmsg, ids = call(first_select_kernel, [pshape, row8], [VMEM] * 2)(arrived, wanted)
    v_raw, beta, ymsg = call(
        first_forward_kernel, [(WANT, BS), row8, (Y * 8, BS)], [VMEM] * 2, **heavy
    )(blocks, exchange(pmsg, PLANE, N_PLANE))
    rows_one, zmsg = call(adjoint_kernel, [row8, zshape], [VMEM] * 2, [msg], **heavy)(blocks, exchange(ymsg, "y", Y))
    (pmsg,) = call(select_kernel, [pshape], [VMEM] * 3)(exchange(zmsg, "z", Z), wanted, ids)
    model_v, model_a, data_u, data_g, alpha, ymsg = call(
        second_forward_kernel,
        [(OWN, BS), (OWN, BS), row4, row4, row8, (N_PLANE * Y * PRODUCTS, BS)],
        [VMEM] * 6,
        [pltpu.VMEM((2 * PRODUCTS, BS), F32)],
        **heavy,
    )(blocks, exchange(pmsg, PLANE, N_PLANE), v_raw, data, beta, rows_one)
    data_q, rmsg = call(
        products_kernel,
        [row4, (Z, BS)],
        [VMEM],
        [pltpu.VMEM((N_PLANE * RB, BS), F32)] * 3 + [pltpu.VMEM((BS, BS), F32)] * 2,
    )(exchange(ymsg, PLANE + ("y",), N_PLANE * Y))
    model, data_dir = call(last_kernel, [(OWN, BS), row4], [VMEM] * 8)(
        exchange(rmsg, "z", Z), beta, alpha, model_v, model_a, data_u, data_g, data_q
    )
    last_adjoint(blocks, ownership[pattern.reshape(-1)], data_dir, model_v)
    return model.reshape(1, OWN * BS), data_dir.reshape(-1)


def solution(mesh):
    split = Mesh(mesh.devices.reshape(X, Z, CORE, Y), ("x", "z", "core", "y"))
    placed = (P("y", ROWS), P(ROWS), P(), P(None, ROWS), P(None, ROWS))
    return jax.shard_map(
        on_device,
        mesh=split,
        in_specs=placed,
        out_specs=(P("y", ROWS), P(ROWS)),
        check_vma=False,
    )
```

```python
import jax
import jax.numpy as jnp
from jax import lax
from jax.experimental import pallas as pl
from jax.experimental.pallas import tpu as pltpu
from jax.sharding import Mesh
from jax.sharding import PartitionSpec as P

EPS = 1e-12
F32 = jnp.float32
BF16 = jnp.bfloat16

X, Z, CORE, Y = 4, 16, 2, 4
ROWS = ("x", "z", "core")
PLANE = ("x", "core")
N_PLANE = X * CORE
N_ROWS = X * Z * CORE

BS = 128
RB = 4
NNZ = 8
ENTRIES = RB * NNZ
OWN = 16
WANT = ENTRIES + OWN
ZCH = ENTRIES + 1
PCH = WANT + 1
PRODUCTS = 12
PART = 4
GROUPS = BS // ENTRIES
DOTS = 9

VMEM = pl.BlockSpec(memory_space=pltpu.VMEM)
SMEM = pl.BlockSpec(memory_space=pltpu.SMEM)
HBM = pl.BlockSpec(memory_space=pltpu.HBM)


def call(kernel, outs, ins, scratch=(), flops=0, moved=0, vmem=32 * 1024 * 1024):
    return pl.pallas_call(
        kernel,
        out_shape=tuple(jax.ShapeDtypeStruct(s, F32) for s in outs),
        in_specs=list(ins),
        out_specs=tuple(VMEM for _ in outs),
        scratch_shapes=list(scratch),
        compiler_params=pltpu.CompilerParams(vmem_limit_bytes=vmem),
        cost_estimate=pl.CostEstimate(flops=flops, bytes_accessed=moved, transcendentals=0),
    )


def two_sum(a, b):
    s = a + b
    bb = s - a
    return s, (a - (s - bb)) + (b - bb)


def halves(a):
    c = a * 4097.0
    high = c - (c - a)
    return high, a - high


def two_prod(a, b):
    p = a * b
    ah, al = halves(a)
    bh, bl = halves(b)
    return p, ((ah * bh - p) + ah * bl + al * bh) + al * bl


def dd_add(a, b):
    s, e = two_sum(a[0], b[0])
    e = e + (a[1] + b[1])
    h = s + e
    return h, e - (h - s)


def dd_mul(a, b):
    p, e = two_prod(a[0], b[0])
    e = e + (a[0] * b[1] + a[1] * b[0])
    h = p + e
    return h, e - (h - p)


def dd_scale(a, f):
    return a[0] * f, a[1] * f


def fold_rows(pair):
    n = pair[0].shape[0]
    while n > 1:
        n //= 2
        pair = dd_add((pair[0][:n], pair[1][:n]), (pair[0][n:], pair[1][n:]))
    return pair


def pick_row(a, i):
    row = a[0:1, :]
    for r in range(1, a.shape[0]):
        row = jnp.where(i == r, a[r : r + 1, :], row)
    return row


def dot_rows(a, b):
    return fold_rows(two_prod(a, b))


def adjoint_terms(block, u_rows, msg, extra):
    for r in range(RB):
        spread = jnp.transpose(jnp.broadcast_to(u_rows[r], (BS, BS)))
        for k in range(NNZ):
            e = r * NNZ + k
            msg[e : e + 1, :] = jnp.sum(block(r, k) * spread, axis=0, keepdims=True)
    msg[ENTRIES : ENTRIES + 1, :] = extra


def spread_message(msg, zmsg):
    whole = msg[0:ZCH, :]
    for z in range(Z):
        zmsg[z * ZCH : (z + 1) * ZCH, :] = whole


def forward_rows(blocks, chosen):
    rows = []
    for r in range(RB):
        total = blocks[r, 0] * chosen[r * NNZ : r * NNZ + 1, :]
        for k in range(1, NNZ):
            e = r * NNZ + k
            total = total + blocks[r, k] * chosen[e : e + 1, :]
        rows.append(jnp.sum(jnp.transpose(total), axis=0, keepdims=True))
    return rows


def first_kernel(
    blocks, seis, signs, pat, own, data, zmsg, named, msg, held, seis_v, signs_v, pat_s, own_s, sems, block_sems
):
    small = [
        pltpu.make_async_copy(src, dst, sems.at[i])
        for i, (src, dst) in enumerate(((pat, pat_s), (own, own_s), (seis, seis_v), (signs, signs_v)))
    ]
    large = [
        pltpu.make_async_copy(blocks.at[pl.ds(r, PART)], held.at[pl.ds(r, PART)], block_sems.at[r // PART])
        for r in range(0, RB, PART)
    ]
    for copy in small + large:
        copy.start()
    small[2].wait()
    small[3].wait()
    signed = (2 * signs_v[...] - 1).astype(F32) * seis_v[...]
    whole = jnp.sum(signed, axis=0, keepdims=True)
    rows = [whole[:, r * BS : (r + 1) * BS] for r in range(RB)]
    for r in range(RB):
        data[r : r + 1, :] = rows[r]
    square = jnp.sum(whole * whole, axis=1, keepdims=True)

    small[0].wait()
    small[1].wait()
    sub = lax.broadcasted_iota(jnp.int32, (ENTRIES, BS), 0)
    lane = lax.broadcasted_iota(jnp.int32, (1, BS), 1) - lax.axis_index("z") % GROUPS * ENTRIES
    col = jnp.zeros((ENTRIES, BS), jnp.int32)
    row = jnp.full((1, BS), -1, jnp.int32)
    for e in range(ENTRIES):
        s = own_s[pat_s[e // NNZ, e % NNZ]]
        col = jnp.where(sub == e, s, col)
        row = jnp.where(lane == e, s, row)
    named[...] = col.astype(F32)
    ids = row.astype(F32)

    def block(r, k):
        if k == 0 and r % PART == 0:
            large[r // PART].wait()
        return held[r, k]

    adjoint_terms(block, rows, msg, jnp.where(ids < 0.0, square, ids))
    spread_message(msg, zmsg)


def select_sum(arrived, ids, wanted, pmsg, extra):
    terms = jnp.concatenate([arrived[z * ZCH : z * ZCH + ENTRIES, :] for z in range(Z)], axis=0)
    high = terms.astype(BF16)
    rest = terms - high.astype(F32)
    mid = rest.astype(BF16)
    low = (rest - mid.astype(F32)).astype(BF16)
    step = lax.broadcasted_iota(jnp.int32, (OWN, BS), 0)
    z_here = lax.axis_index("z")
    names = []
    for x in range(X):
        for core in range(CORE):
            i = x * CORE + core
            names.append(wanted[i * ENTRIES : (i + 1) * ENTRIES, :])
            names.append((((x * Z + z_here) * CORE + core) * OWN + step).astype(F32))
    names = jnp.concatenate(names, axis=0)
    pick = jnp.concatenate(
        [jnp.where(names == ids[t : t + 1, :], 1.0, 0.0).astype(BF16) for t in range(Z * ENTRIES // BS)], axis=1
    )
    sums = jnp.dot(pick, low, preferred_element_type=F32)
    both = jnp.dot(pick, jnp.concatenate([mid, high], axis=1), preferred_element_type=F32)
    sums = sums + both[:, :BS] + both[:, BS:]
    for i in range(N_PLANE):
        to = i % CORE * X + i // CORE
        pmsg[to * PCH : to * PCH + WANT, :] = sums[i * WANT : (i + 1) * WANT]
        pmsg[to * PCH + WANT : (to + 1) * PCH, :] = extra[0:1, :]


def first_select_kernel(arrived, wanted, pmsg, ids):
    lane = lax.broadcasted_iota(jnp.int32, (1, BS), 1)
    extra = jnp.zeros((1, BS), F32)
    for t in range(Z // GROUPS):
        row = jnp.zeros((1, BS), F32)
        for j in range(GROUPS):
            at = (t * GROUPS + j) * ZCH + ENTRIES
            line = arrived[at : at + 1, :]
            row = jnp.where(lane // ENTRIES == j, line, row)
            extra = extra + jnp.where(lane == (j + 1) % GROUPS * ENTRIES, line, 0.0)
        ids[t : t + 1, :] = row
    ids[Z // GROUPS : 8, :] = jnp.zeros((8 - Z // GROUPS, BS), F32)
    select_sum(arrived, ids, wanted, pmsg, jnp.broadcast_to(extra, (8, BS)))


def select_kernel(arrived, wanted, ids, pmsg):
    extra = arrived[ENTRIES : ENTRIES + 1, :]
    for z in range(1, Z):
        extra = extra + arrived[z * ZCH + ENTRIES : z * ZCH + ZCH, :]
    select_sum(arrived, ids, wanted, pmsg, jnp.broadcast_to(extra, (8, BS)))


def plane_sum(arrived):
    total = arrived[0:WANT, :]
    for i in range(1, N_PLANE):
        total = total + arrived[i * PCH : i * PCH + WANT, :]
    return total


def plane_extra(arrived):
    total = arrived[WANT : WANT + 1, :]
    for i in range(1, N_PLANE):
        total = total + arrived[i * PCH + WANT : i * PCH + WANT + 1, :]
    return jnp.sum(total, axis=1, keepdims=True)


def first_forward_kernel(blocks, arrived, v_raw, beta, ymsg):
    beta_one = jnp.sqrt(plane_extra(arrived) + EPS)
    v = plane_sum(arrived) / beta_one
    v_raw[...] = v
    beta[...] = jnp.broadcast_to(beta_one, (8, BS))
    rows = forward_rows(blocks, v)
    own = v[ENTRIES:WANT]
    extra = jnp.sum(own * own, axis=0, keepdims=True)
    for y in range(Y):
        for r in range(RB):
            ymsg[y * 8 + r : y * 8 + r + 1, :] = rows[r]
        ymsg[y * 8 + RB : (y + 1) * 8, :] = jnp.broadcast_to(extra, (8 - RB, BS))


def adjoint_kernel(blocks, arrived, rows_out, zmsg, msg):
    total = arrived[0:8, :]
    for y in range(1, Y):
        total = total + arrived[y * 8 : (y + 1) * 8, :]
    rows_out[...] = total
    rows = [total[r : r + 1, :] for r in range(RB)]
    adjoint_terms(lambda r, k: blocks[r, k], rows, msg, total[RB : RB + 1, :])
    spread_message(msg, zmsg)


def second_forward_kernel(
    blocks, arrived, v_raw, data, beta, rows_one, model_v, model_a, data_u, data_g, alpha, ymsg, msg
):
    alpha_one = jnp.sqrt(plane_extra(arrived) + EPS)
    v = v_raw[...]
    a = plane_sum(arrived) / alpha_one - alpha_one * v
    g = rows_one[0:RB, :] / alpha_one
    data_g[...] = g
    u = g - alpha_one * (data[...] / beta[0:1, 0:1])
    data_u[...] = u
    alpha[...] = jnp.broadcast_to(alpha_one, (8, BS))
    rows = forward_rows(blocks, a)
    a_own = a[ENTRIES:WANT]
    v_own = v[ENTRIES:WANT] / alpha_one
    model_a[...] = a_own
    model_v[...] = v_own
    for r in range(RB):
        msg[r : r + 1, :] = rows[r]
    y = lax.axis_index("y")
    msg[RB : RB + 1, :] = pick_row(g, y)
    msg[RB + 1 : RB + 2, :] = pick_row(u, y)
    for i, pair in enumerate((dot_rows(a_own, a_own), dot_rows(a_own, v_own), dot_rows(v_own, v_own))):
        msg[RB + 2 + i : RB + 3 + i, :] = pair[0]
        msg[RB + 5 + i : RB + 6 + i, :] = pair[1]
    msg[PRODUCTS : 2 * PRODUCTS, :] = msg[0:PRODUCTS, :]
    whole = msg[...]
    for i in range(N_PLANE * Y // 2):
        ymsg[i * 2 * PRODUCTS : (i + 1) * 2 * PRODUCTS, :] = whole


def products_kernel(arrived, data_q, rmsg, q_all, g_all, u_all, high, low):
    here = lax.axis_index("x") * CORE + lax.axis_index("core")
    mine = jnp.zeros((RB, BS), F32)
    model = []
    for i in range(N_PLANE):
        at = i * Y * PRODUCTS
        q = arrived[at : at + RB, :]
        for y in range(1, Y):
            q = q + arrived[at + y * PRODUCTS : at + y * PRODUCTS + RB, :]
        mine = jnp.where(here == i, q, mine)
        q_all[i * RB : (i + 1) * RB, :] = q
        for y in range(Y):
            source = at + y * PRODUCTS + RB
            g_all[i * RB + y : i * RB + y + 1, :] = arrived[source : source + 1, :]
            u_all[i * RB + y : i * RB + y + 1, :] = arrived[source + 1 : source + 2, :]
            model.append((arrived[source + 2 : source + 5, :], arrived[source + 5 : source + 8, :]))
    data_q[...] = mine
    q = q_all[...]
    u = u_all[...]
    g = g_all[...]
    pairs = [dot_rows(u, u), dot_rows(q, q), dot_rows(q, g), dot_rows(q, u), dot_rows(g, g), dot_rows(g, u)]
    high[...] = jnp.zeros((BS, BS), F32)
    low[...] = jnp.zeros((BS, BS), F32)
    for i, pair in enumerate(pairs):
        high[i : i + 1, :] = pair[0]
        low[i : i + 1, :] = pair[1]
    while len(model) > 1:
        model = [dd_add(model[i], model[i + 1]) for i in range(0, len(model), 2)]
    high[6:9, :] = model[0][0]
    low[6:9, :] = model[0][1]
    pair = fold_rows((jnp.transpose(high[...]), jnp.transpose(low[...])))
    line = pair[0] + pltpu.roll(pair[1], BS // 2, 1)
    rmsg[...] = jnp.broadcast_to(line, (Z, BS))


def last_kernel(arrived, beta, alpha, model_v, model_a, data_u, data_g, data_q, model, data_dir):
    total = arrived[...]
    pair = fold_rows((total, jnp.zeros_like(total)))
    lane = lax.broadcasted_iota(jnp.int32, (1, BS), 1)

    rest = jnp.where(lane < BS // 2, pair[1], pair[0] + pair[1])

    def dot(i):
        top = jnp.sum(jnp.where(lane == i, pair[0], 0.0), axis=1, keepdims=True)
        low = jnp.sum(jnp.where(lane % (BS // 2) == i, rest, 0.0), axis=1, keepdims=True)
        return two_sum(top, low)

    uu, qq, qg, qu, gg, gu, aa, av, vv = [dot(i) for i in range(DOTS)]
    beta_one = beta[0:1, 0:1]
    alpha_one = alpha[0:1, 0:1]
    beta_two = jnp.sqrt(uu[0] + EPS)
    b_sq = two_prod(beta_two, beta_two)
    square = dd_add(dd_mul(b_sq, dd_add(dd_mul(b_sq, vv), dd_scale(av, -2.0))), aa)
    square = jnp.maximum(square[0] / b_sq[0], 0.0)
    alpha_two = jnp.sqrt(square + EPS)
    a_sq = two_prod(alpha_two, alpha_two)
    part = dd_add(dd_mul(b_sq, dd_add(dd_mul(b_sq, gg), dd_scale(qg, -2.0))), qq)
    part = dd_add(part, dd_mul(a_sq, dd_add(dd_mul(a_sq, uu), dd_scale(qu, -2.0))))
    part = dd_add(part, dd_scale(dd_mul(dd_mul(a_sq, b_sq), gu), 2.0))
    scale = beta_two * alpha_two
    square = jnp.maximum(part[0], 0.0) / scale / scale
    beta_three = jnp.sqrt(square + EPS)

    rho = jnp.sqrt(alpha_one * alpha_one + beta_two * beta_two)
    cosine = alpha_one / rho
    sine = beta_two / rho
    theta = sine * alpha_two
    rhobar = -cosine * alpha_two
    phi = cosine * beta_one
    phibar = sine * beta_one
    v_one = model_v[...]
    v_two = (model_a[...] / beta_two - beta_two * v_one) / alpha_two
    found = phi / rho * v_one
    w = v_two - theta / rho * v_one
    rho = jnp.sqrt(rhobar * rhobar + beta_three * beta_three)
    phi = rhobar / rho * phibar
    model[...] = found + phi / rho * w
    u_three = (data_q[...] - b_sq[0] * data_g[...] - a_sq[0] * data_u[...]) / scale
    data_dir[...] = u_three / beta_three


def exchange(array, axes, peers):
    n = array.shape[0] // peers
    if n % 8 == 0:
        return lax.all_to_all(array.reshape(peers, n, BS), axes, 0, 0, tiled=True).reshape(array.shape)
    return lax.all_to_all(array.reshape(peers * n, 1, BS), axes, 0, 0, tiled=True).reshape(array.shape)


def last_adjoint(blocks, slot, u_vec, v_vec):
    terms = jnp.einsum("rkij,ri->rkj", blocks, u_vec, precision=lax.Precision.HIGHEST)
    targets = lax.broadcasted_iota(jnp.int32, (OWN * N_ROWS, 1), 0)
    pick = (targets == slot[None, :]).astype(F32)
    total = jnp.dot(pick, terms.reshape(ENTRIES, BS), precision=lax.Precision.HIGHEST)
    v_vec = lax.psum_scatter(total, ROWS, scatter_dimension=0, tiled=True) - v_vec
    return v_vec, jnp.sqrt(lax.psum(jnp.sum(v_vec * v_vec), ROWS + ("y",)) + EPS)


def on_device(frechet, pattern, ownership, seismograms, signs):
    blocks = frechet[0]
    size = blocks.size
    msg = pltpu.VMEM((ENTRIES + 8, BS), F32)
    row4, row8 = (RB, BS), (8, BS)
    zshape, pshape = (Z * ZCH, BS), (N_PLANE * PCH, BS)
    heavy = dict(flops=2 * size, moved=4 * size)

    data, zmsg, named = call(
        first_kernel,
        [row4, zshape, (ENTRIES, BS)],
        [HBM] * 5,
        [
            msg,
            pltpu.VMEM(blocks.shape, F32),
            pltpu.VMEM(seismograms.shape, F32),
            pltpu.VMEM(signs.shape, jnp.int32),
            pltpu.SMEM(pattern.shape, jnp.int32),
            pltpu.SMEM(ownership.shape, jnp.int32),
            pltpu.SemaphoreType.DMA((4,)),
            pltpu.SemaphoreType.DMA((RB // PART,)),
        ],
        vmem=59 * 1024 * 1024,
        **heavy,
    )(blocks, seismograms, signs, pattern, ownership)
    arrived = exchange(zmsg, "z", Z)
    wanted = lax.all_gather(named, PLANE, axis=0, tiled=True)
    pmsg, ids = call(first_select_kernel, [pshape, row8], [VMEM] * 2)(arrived, wanted)
    v_raw, beta, ymsg = call(
        first_forward_kernel, [(WANT, BS), row8, (Y * 8, BS)], [VMEM] * 2, **heavy
    )(blocks, exchange(pmsg, ("core", "x"), N_PLANE))
    rows_one, zmsg = call(adjoint_kernel, [row8, zshape], [VMEM] * 2, [msg], **heavy)(blocks, exchange(ymsg, "y", Y))
    (pmsg,) = call(select_kernel, [pshape], [VMEM] * 3)(exchange(zmsg, "z", Z), wanted, ids)
    model_v, model_a, data_u, data_g, alpha, ymsg = call(
        second_forward_kernel,
        [(OWN, BS), (OWN, BS), row4, row4, row8, (N_PLANE * Y * PRODUCTS, BS)],
        [VMEM] * 6,
        [pltpu.VMEM((2 * PRODUCTS, BS), F32)],
        **heavy,
    )(blocks, exchange(pmsg, ("core", "x"), N_PLANE), v_raw, data, beta, rows_one)
    data_q, rmsg = call(
        products_kernel,
        [row4, (Z, BS)],
        [VMEM],
        [pltpu.VMEM((N_PLANE * RB, BS), F32)] * 3 + [pltpu.VMEM((BS, BS), F32)] * 2,
    )(exchange(ymsg, PLANE + ("y",), N_PLANE * Y))
    model, data_dir = call(last_kernel, [(OWN, BS), row4], [VMEM] * 8)(
        exchange(rmsg, "z", Z), beta, alpha, model_v, model_a, data_u, data_g, data_q
    )
    last_adjoint(blocks, ownership[pattern.reshape(-1)], data_dir, model_v)
    return model.reshape(1, OWN * BS), data_dir.reshape(-1)


def solution(mesh):
    split = Mesh(mesh.devices.reshape(X, Z, CORE, Y), ("x", "z", "core", "y"))
    placed = (P("y", ROWS), P(ROWS), P(), P(None, ROWS), P(None, ROWS))
    return jax.shard_map(
        on_device,
        mesh=split,
        in_specs=placed,
        out_specs=(P("y", ROWS), P(ROWS)),
        check_vma=False,
    )
```

```python
import jax
import jax.numpy as jnp
from jax import lax
from jax.experimental import pallas as pl
from jax.experimental.pallas import tpu as pltpu
from jax.sharding import Mesh
from jax.sharding import PartitionSpec as P

EPS = 1e-12
F32 = jnp.float32
BF16 = jnp.bfloat16

X, Z, CORE, Y = 4, 16, 2, 4
ROWS = ("x", "z", "core")
PLANE = ("x", "core")
N_PLANE = X * CORE
N_ROWS = X * Z * CORE

BS = 128
RB = 4
NNZ = 8
ENTRIES = RB * NNZ
OWN = 16
WANT = ENTRIES + OWN
ZCH = ENTRIES + 1
PCH = WANT + 1
PRODUCTS = 12
PART = 2
GROUPS = BS // ENTRIES
DOTS = 9

VMEM = pl.BlockSpec(memory_space=pltpu.VMEM)
SMEM = pl.BlockSpec(memory_space=pltpu.SMEM)
HBM = pl.BlockSpec(memory_space=pltpu.HBM)


def call(kernel, outs, ins, scratch=(), flops=0, moved=0, vmem=32 * 1024 * 1024):
    return pl.pallas_call(
        kernel,
        out_shape=tuple(jax.ShapeDtypeStruct(s, F32) for s in outs),
        in_specs=list(ins),
        out_specs=tuple(VMEM for _ in outs),
        scratch_shapes=list(scratch),
        compiler_params=pltpu.CompilerParams(vmem_limit_bytes=vmem),
        cost_estimate=pl.CostEstimate(flops=flops, bytes_accessed=moved, transcendentals=0),
    )


def two_sum(a, b):
    s = a + b
    bb = s - a
    return s, (a - (s - bb)) + (b - bb)


def halves(a):
    c = a * 4097.0
    high = c - (c - a)
    return high, a - high


def two_prod(a, b):
    p = a * b
    ah, al = halves(a)
    bh, bl = halves(b)
    return p, ((ah * bh - p) + ah * bl + al * bh) + al * bl


def dd_add(a, b):
    s, e = two_sum(a[0], b[0])
    e = e + (a[1] + b[1])
    h = s + e
    return h, e - (h - s)


def dd_mul(a, b):
    p, e = two_prod(a[0], b[0])
    e = e + (a[0] * b[1] + a[1] * b[0])
    h = p + e
    return h, e - (h - p)


def dd_scale(a, f):
    return a[0] * f, a[1] * f


def fold_rows(pair):
    n = pair[0].shape[0]
    while n > 1:
        n //= 2
        pair = dd_add((pair[0][:n], pair[1][:n]), (pair[0][n:], pair[1][n:]))
    return pair


def pick_row(a, i):
    row = a[0:1, :]
    for r in range(1, a.shape[0]):
        row = jnp.where(i == r, a[r : r + 1, :], row)
    return row


def dot_rows(a, b):
    return fold_rows(two_prod(a, b))


def adjoint_terms(block, u_rows, msg, extra):
    for r in range(RB):
        spread = jnp.transpose(jnp.broadcast_to(u_rows[r], (BS, BS)))
        for k in range(NNZ):
            e = r * NNZ + k
            msg[e : e + 1, :] = jnp.sum(block(r, k) * spread, axis=0, keepdims=True)
    msg[ENTRIES : ENTRIES + 1, :] = extra


def spread_message(msg, zmsg):
    whole = msg[0:ZCH, :]
    for z in range(Z):
        zmsg[z * ZCH : (z + 1) * ZCH, :] = whole


def forward_rows(blocks, chosen):
    rows = []
    for r in range(RB):
        total = blocks[r, 0] * chosen[r * NNZ : r * NNZ + 1, :]
        for k in range(1, NNZ):
            e = r * NNZ + k
            total = total + blocks[r, k] * chosen[e : e + 1, :]
        rows.append(jnp.sum(jnp.transpose(total), axis=0, keepdims=True))
    return rows


def first_kernel(
    blocks, seis, signs, pat, own, data, zmsg, named, msg, held, seis_v, signs_v, pat_s, own_s, sems, block_sems
):
    small = [
        pltpu.make_async_copy(src, dst, sems.at[i])
        for i, (src, dst) in enumerate(((pat, pat_s), (own, own_s), (seis, seis_v), (signs, signs_v)))
    ]
    large = [
        pltpu.make_async_copy(blocks.at[pl.ds(r, PART)], held.at[pl.ds(r, PART)], block_sems.at[r // PART])
        for r in range(0, RB, PART)
    ]
    for copy in small + large:
        copy.start()
    small[2].wait()
    small[3].wait()
    signed = (2 * signs_v[...] - 1).astype(F32) * seis_v[...]
    whole = jnp.sum(signed, axis=0, keepdims=True)
    rows = [whole[:, r * BS : (r + 1) * BS] for r in range(RB)]
    for r in range(RB):
        data[r : r + 1, :] = rows[r]
    square = jnp.sum(whole * whole, axis=1, keepdims=True)

    small[0].wait()
    small[1].wait()
    sub = lax.broadcasted_iota(jnp.int32, (ENTRIES, BS), 0)
    lane = lax.broadcasted_iota(jnp.int32, (1, BS), 1) - lax.axis_index("z") % GROUPS * ENTRIES
    col = jnp.zeros((ENTRIES, BS), jnp.int32)
    row = jnp.full((1, BS), -1, jnp.int32)
    for e in range(ENTRIES):
        s = own_s[pat_s[e // NNZ, e % NNZ]]
        col = jnp.where(sub == e, s, col)
        row = jnp.where(lane == e, s, row)
    named[...] = col.astype(F32)
    ids = row.astype(F32)

    def block(r, k):
        if k == 0 and r % PART == 0:
            large[r // PART].wait()
        return held[r, k]

    adjoint_terms(block, rows, msg, jnp.where(ids < 0.0, square, ids))
    spread_message(msg, zmsg)


def select_sum(arrived, ids, wanted, pmsg, extra):
    terms = jnp.concatenate([arrived[z * ZCH : z * ZCH + ENTRIES, :] for z in range(Z)], axis=0)
    high = terms.astype(BF16)
    rest = terms - high.astype(F32)
    mid = rest.astype(BF16)
    low = (rest - mid.astype(F32)).astype(BF16)
    step = lax.broadcasted_iota(jnp.int32, (OWN, BS), 0)
    z_here = lax.axis_index("z")
    names = []
    for x in range(X):
        for core in range(CORE):
            i = x * CORE + core
            names.append(wanted[i * ENTRIES : (i + 1) * ENTRIES, :])
            names.append((((x * Z + z_here) * CORE + core) * OWN + step).astype(F32))
    names = jnp.concatenate(names, axis=0)
    pick = jnp.concatenate(
        [jnp.where(names == ids[t : t + 1, :], 1.0, 0.0).astype(BF16) for t in range(Z * ENTRIES // BS)], axis=1
    )
    sums = jnp.dot(pick, low, preferred_element_type=F32)
    both = jnp.dot(pick, jnp.concatenate([mid, high], axis=1), preferred_element_type=F32)
    sums = sums + both[:, :BS] + both[:, BS:]
    for i in range(N_PLANE):
        to = i % CORE * X + i // CORE
        pmsg[to * PCH : to * PCH + WANT, :] = sums[i * WANT : (i + 1) * WANT]
        pmsg[to * PCH + WANT : (to + 1) * PCH, :] = extra[0:1, :]


def first_select_kernel(arrived, wanted, pmsg, ids):
    lane = lax.broadcasted_iota(jnp.int32, (1, BS), 1)
    extra = jnp.zeros((1, BS), F32)
    for t in range(Z // GROUPS):
        row = jnp.zeros((1, BS), F32)
        for j in range(GROUPS):
            at = (t * GROUPS + j) * ZCH + ENTRIES
            line = arrived[at : at + 1, :]
            row = jnp.where(lane // ENTRIES == j, line, row)
            extra = extra + jnp.where(lane == (j + 1) % GROUPS * ENTRIES, line, 0.0)
        ids[t : t + 1, :] = row
    ids[Z // GROUPS : 8, :] = jnp.zeros((8 - Z // GROUPS, BS), F32)
    select_sum(arrived, ids, wanted, pmsg, jnp.broadcast_to(extra, (8, BS)))


def select_kernel(arrived, wanted, ids, pmsg):
    extra = arrived[ENTRIES : ENTRIES + 1, :]
    for z in range(1, Z):
        extra = extra + arrived[z * ZCH + ENTRIES : z * ZCH + ZCH, :]
    select_sum(arrived, ids, wanted, pmsg, jnp.broadcast_to(extra, (8, BS)))


def plane_sum(arrived):
    total = arrived[0:WANT, :]
    for i in range(1, N_PLANE):
        total = total + arrived[i * PCH : i * PCH + WANT, :]
    return total


def plane_extra(arrived):
    total = arrived[WANT : WANT + 1, :]
    for i in range(1, N_PLANE):
        total = total + arrived[i * PCH + WANT : i * PCH + WANT + 1, :]
    return jnp.sum(total, axis=1, keepdims=True)


def first_forward_kernel(blocks, arrived, v_raw, beta, ymsg):
    beta_one = jnp.sqrt(plane_extra(arrived) + EPS)
    v = plane_sum(arrived) / beta_one
    v_raw[...] = v
    beta[...] = jnp.broadcast_to(beta_one, (8, BS))
    rows = forward_rows(blocks, v)
    own = v[ENTRIES:WANT]
    extra = jnp.sum(own * own, axis=0, keepdims=True)
    for y in range(Y):
        for r in range(RB):
            ymsg[y * 8 + r : y * 8 + r + 1, :] = rows[r]
        ymsg[y * 8 + RB : (y + 1) * 8, :] = jnp.broadcast_to(extra, (8 - RB, BS))


def adjoint_kernel(blocks, arrived, rows_out, zmsg, msg):
    total = arrived[0:8, :]
    for y in range(1, Y):
        total = total + arrived[y * 8 : (y + 1) * 8, :]
    rows_out[...] = total
    rows = [total[r : r + 1, :] for r in range(RB)]
    adjoint_terms(lambda r, k: blocks[r, k], rows, msg, total[RB : RB + 1, :])
    spread_message(msg, zmsg)


def second_forward_kernel(
    blocks, arrived, v_raw, data, beta, rows_one, model_v, model_a, data_u, data_g, alpha, ymsg, msg
):
    alpha_one = jnp.sqrt(plane_extra(arrived) + EPS)
    v = v_raw[...]
    a = plane_sum(arrived) / alpha_one - alpha_one * v
    g = rows_one[0:RB, :] / alpha_one
    data_g[...] = g
    u = g - alpha_one * (data[...] / beta[0:1, 0:1])
    data_u[...] = u
    alpha[...] = jnp.broadcast_to(alpha_one, (8, BS))
    rows = forward_rows(blocks, a)
    a_own = a[ENTRIES:WANT]
    v_own = v[ENTRIES:WANT] / alpha_one
    model_a[...] = a_own
    model_v[...] = v_own
    for r in range(RB):
        msg[r : r + 1, :] = rows[r]
    y = lax.axis_index("y")
    msg[RB : RB + 1, :] = pick_row(g, y)
    msg[RB + 1 : RB + 2, :] = pick_row(u, y)
    for i, pair in enumerate((dot_rows(a_own, a_own), dot_rows(a_own, v_own), dot_rows(v_own, v_own))):
        msg[RB + 2 + i : RB + 3 + i, :] = pair[0]
        msg[RB + 5 + i : RB + 6 + i, :] = pair[1]
    msg[PRODUCTS : 2 * PRODUCTS, :] = msg[0:PRODUCTS, :]
    whole = msg[...]
    for i in range(N_PLANE * Y // 2):
        ymsg[i * 2 * PRODUCTS : (i + 1) * 2 * PRODUCTS, :] = whole


def products_kernel(arrived, data_q, rmsg, q_all, g_all, u_all, high, low):
    here = lax.axis_index("x") * CORE + lax.axis_index("core")
    mine = jnp.zeros((RB, BS), F32)
    model = []
    for i in range(N_PLANE):
        at = i * Y * PRODUCTS
        q = arrived[at : at + RB, :]
        for y in range(1, Y):
            q = q + arrived[at + y * PRODUCTS : at + y * PRODUCTS + RB, :]
        mine = jnp.where(here == i, q, mine)
        q_all[i * RB : (i + 1) * RB, :] = q
        for y in range(Y):
            source = at + y * PRODUCTS + RB
            g_all[i * RB + y : i * RB + y + 1, :] = arrived[source : source + 1, :]
            u_all[i * RB + y : i * RB + y + 1, :] = arrived[source + 1 : source + 2, :]
            model.append((arrived[source + 2 : source + 5, :], arrived[source + 5 : source + 8, :]))
    data_q[...] = mine
    q = q_all[...]
    u = u_all[...]
    g = g_all[...]
    pairs = [dot_rows(u, u), dot_rows(q, q), dot_rows(q, g), dot_rows(q, u), dot_rows(g, g), dot_rows(g, u)]
    high[...] = jnp.zeros((BS, BS), F32)
    low[...] = jnp.zeros((BS, BS), F32)
    for i, pair in enumerate(pairs):
        high[i : i + 1, :] = pair[0]
        low[i : i + 1, :] = pair[1]
    while len(model) > 1:
        model = [dd_add(model[i], model[i + 1]) for i in range(0, len(model), 2)]
    high[6:9, :] = model[0][0]
    low[6:9, :] = model[0][1]
    pair = fold_rows((jnp.transpose(high[...]), jnp.transpose(low[...])))
    line = pair[0] + pltpu.roll(pair[1], BS // 2, 1)
    rmsg[...] = jnp.broadcast_to(line, (Z, BS))


def last_kernel(arrived, beta, alpha, model_v, model_a, data_u, data_g, data_q, model, data_dir):
    total = arrived[...]
    pair = fold_rows((total, jnp.zeros_like(total)))
    lane = lax.broadcasted_iota(jnp.int32, (1, BS), 1)

    rest = jnp.where(lane < BS // 2, pair[1], pair[0] + pair[1])

    def dot(i):
        top = jnp.sum(jnp.where(lane == i, pair[0], 0.0), axis=1, keepdims=True)
        low = jnp.sum(jnp.where(lane % (BS // 2) == i, rest, 0.0), axis=1, keepdims=True)
        return two_sum(top, low)

    uu, qq, qg, qu, gg, gu, aa, av, vv = [dot(i) for i in range(DOTS)]
    beta_one = beta[0:1, 0:1]
    alpha_one = alpha[0:1, 0:1]
    beta_two = jnp.sqrt(uu[0] + EPS)
    b_sq = two_prod(beta_two, beta_two)
    square = dd_add(dd_mul(b_sq, dd_add(dd_mul(b_sq, vv), dd_scale(av, -2.0))), aa)
    square = jnp.maximum(square[0] / b_sq[0], 0.0)
    alpha_two = jnp.sqrt(square + EPS)
    a_sq = two_prod(alpha_two, alpha_two)
    part = dd_add(dd_mul(b_sq, dd_add(dd_mul(b_sq, gg), dd_scale(qg, -2.0))), qq)
    part = dd_add(part, dd_mul(a_sq, dd_add(dd_mul(a_sq, uu), dd_scale(qu, -2.0))))
    part = dd_add(part, dd_scale(dd_mul(dd_mul(a_sq, b_sq), gu), 2.0))
    scale = beta_two * alpha_two
    square = jnp.maximum(part[0], 0.0) / scale / scale
    beta_three = jnp.sqrt(square + EPS)

    rho = jnp.sqrt(alpha_one * alpha_one + beta_two * beta_two)
    cosine = alpha_one / rho
    sine = beta_two / rho
    theta = sine * alpha_two
    rhobar = -cosine * alpha_two
    phi = cosine * beta_one
    phibar = sine * beta_one
    v_one = model_v[...]
    v_two = (model_a[...] / beta_two - beta_two * v_one) / alpha_two
    found = phi / rho * v_one
    w = v_two - theta / rho * v_one
    rho = jnp.sqrt(rhobar * rhobar + beta_three * beta_three)
    phi = rhobar / rho * phibar
    model[...] = found + phi / rho * w
    u_three = (data_q[...] - b_sq[0] * data_g[...] - a_sq[0] * data_u[...]) / scale
    data_dir[...] = u_three / beta_three


def exchange(array, axes, peers):
    n = array.shape[0] // peers
    if n % 8 == 0:
        return lax.all_to_all(array.reshape(peers, n, BS), axes, 0, 0, tiled=True).reshape(array.shape)
    return lax.all_to_all(array.reshape(peers * n, 1, BS), axes, 0, 0, tiled=True).reshape(array.shape)


def last_adjoint(blocks, slot, u_vec, v_vec):
    terms = jnp.einsum("rkij,ri->rkj", blocks, u_vec, precision=lax.Precision.HIGHEST)
    targets = lax.broadcasted_iota(jnp.int32, (OWN * N_ROWS, 1), 0)
    pick = (targets == slot[None, :]).astype(F32)
    total = jnp.dot(pick, terms.reshape(ENTRIES, BS), precision=lax.Precision.HIGHEST)
    v_vec = lax.psum_scatter(total, ROWS, scatter_dimension=0, tiled=True) - v_vec
    return v_vec, jnp.sqrt(lax.psum(jnp.sum(v_vec * v_vec), ROWS + ("y",)) + EPS)


def on_device(frechet, pattern, ownership, seismograms, signs):
    blocks = frechet[0]
    size = blocks.size
    msg = pltpu.VMEM((ENTRIES + 8, BS), F32)
    row4, row8 = (RB, BS), (8, BS)
    zshape, pshape = (Z * ZCH, BS), (N_PLANE * PCH, BS)
    heavy = dict(flops=2 * size, moved=4 * size)

    data, zmsg, named = call(
        first_kernel,
        [row4, zshape, (ENTRIES, BS)],
        [HBM] * 5,
        [
            msg,
            pltpu.VMEM(blocks.shape, F32),
            pltpu.VMEM(seismograms.shape, F32),
            pltpu.VMEM(signs.shape, jnp.int32),
            pltpu.SMEM(pattern.shape, jnp.int32),
            pltpu.SMEM(ownership.shape, jnp.int32),
            pltpu.SemaphoreType.DMA((4,)),
            pltpu.SemaphoreType.DMA((RB // PART,)),
        ],
        vmem=59 * 1024 * 1024,
        **heavy,
    )(blocks, seismograms, signs, pattern, ownership)
    arrived = exchange(zmsg, "z", Z)
    wanted = lax.all_gather(named, PLANE, axis=0, tiled=True)
    pmsg, ids = call(first_select_kernel, [pshape, row8], [VMEM] * 2)(arrived, wanted)
    v_raw, beta, ymsg = call(
        first_forward_kernel, [(WANT, BS), row8, (Y * 8, BS)], [VMEM] * 2, **heavy
    )(blocks, exchange(pmsg, ("core", "x"), N_PLANE))
    rows_one, zmsg = call(adjoint_kernel, [row8, zshape], [VMEM] * 2, [msg], **heavy)(blocks, exchange(ymsg, "y", Y))
    (pmsg,) = call(select_kernel, [pshape], [VMEM] * 3)(exchange(zmsg, "z", Z), wanted, ids)
    model_v, model_a, data_u, data_g, alpha, ymsg = call(
        second_forward_kernel,
        [(OWN, BS), (OWN, BS), row4, row4, row8, (N_PLANE * Y * PRODUCTS, BS)],
        [VMEM] * 6,
        [pltpu.VMEM((2 * PRODUCTS, BS), F32)],
        **heavy,
    )(blocks, exchange(pmsg, ("core", "x"), N_PLANE), v_raw, data, beta, rows_one)
    data_q, rmsg = call(
        products_kernel,
        [row4, (Z, BS)],
        [VMEM],
        [pltpu.VMEM((N_PLANE * RB, BS), F32)] * 3 + [pltpu.VMEM((BS, BS), F32)] * 2,
    )(exchange(ymsg, PLANE + ("y",), N_PLANE * Y))
    model, data_dir = call(last_kernel, [(OWN, BS), row4], [VMEM] * 8)(
        exchange(rmsg, "z", Z), beta, alpha, model_v, model_a, data_u, data_g, data_q
    )
    last_adjoint(blocks, ownership[pattern.reshape(-1)], data_dir, model_v)
    return model.reshape(1, OWN * BS), data_dir.reshape(-1)


def solution(mesh):
    split = Mesh(mesh.devices.reshape(X, Z, CORE, Y), ("x", "z", "core", "y"))
    placed = (P("y", ROWS), P(ROWS), P(), P(None, ROWS), P(None, ROWS))
    return jax.shard_map(
        on_device,
        mesh=split,
        in_specs=placed,
        out_specs=(P("y", ROWS), P(ROWS)),
        check_vma=False,
    )
```
